128 devices in a mesh: horiz: 16 (over z, y), depth: 8 (over x, core).
Axes of the slice: x: 4, y: 4, z: 4, core: 2. Of those that a mesh axis runs over, the one named last changes fastest.
Arguments:
- source_field: float32 [64, 512, 512], P('depth', 'horiz'), may hold values from -6 to 6
- methane: float32 [64, 512, 512], P('depth', 'horiz'), may hold values from 0.2 to 1.5
- sulfate: float32 [64, 512, 512], P('depth', 'horiz'), may hold values from 0.2 to 1.5
- layer_of_cell: int32 [64], replicated, may hold values from 0 to 7
- perm_horizontal: float32 [8], replicated, may hold values from 0.3 to 3
- perm_vertical: float32 [8], replicated, may hold values from 0.3 to 3
- vent_mask: int32 [512, 512], P('horiz'), may hold values 0 or 1
Outputs:
- pressure: float32 [64, 512, 512], P('depth', 'horiz')
- methane_out: float32 [64, 512, 512], P('depth', 'horiz')
- sulfate_out: float32 [64, 512, 512], P('depth', 'horiz')
The draws below stay inside these ranges and needn't reach their ends.
All inputs are finite; a program needn't handle non-finite values. No bound on the sum of `vent_mask` on one device may be relied on, other than what follows from the above.
Results may differ from the reference program's by a relative error of at most 0.0003.
Values sent between devices are 32-bit elements; how exact they have to be, the bound alone decides.
A program may use at most 64 MiB of HBM per device.

```python
import math
import jax
import jax.numpy as jnp
from jax import lax

NX = 512
NY = 512
LAYERS = 8
STEPS = 4
NZ = 64


def set_ends(drawn, rng, smallest, top_value):
    place = [jax.random.randint(jax.random.fold_in(rng, axis), (), 0, length) for axis, length in enumerate(drawn.shape)]
    widest = drawn.shape.index(max(drawn.shape))
    next_to = place[:widest] + [(place[widest] + 1) % drawn.shape[widest]] + place[widest + 1:]
    return drawn.at[tuple(place)].set(smallest).at[tuple(next_to)].set(top_value)


def block_scale(own_key, shape, pieces, low, top_value):
    gain = 1.0
    for position, blocks in pieces:
        heights = jax.random.uniform(jax.random.fold_in(jax.random.fold_in(own_key, 6), position), (blocks,), jnp.float32, low / len(pieces), top_value / len(pieces))
        gain = gain * jnp.repeat(jnp.exp(heights), shape[position] // blocks).reshape((-1,) + (1,) * (len(shape) - 1 - position))
    return gain


def bell_draw(rng, dims, spread, most, split=(), kind=jnp.bfloat16):
    array = spread * jax.random.normal(rng, dims, jnp.float32)
    if split:
        array = array * block_scale(rng, dims, split, -0.22, 0.18)
    return jnp.clip(array, -most, most).astype(kind)


def setup_inputs(seed: int = 0) -> dict:
    seeds = jax.random.split(jax.random.key(seed), 8)
    return {
        "source_field": bell_draw(seeds[0], (NZ, NX, NY), 1.0, 6.0, ((0, 8), (1, 16)), jnp.float32),
        "methane": jnp.clip(0.2 + 1.3 * jax.random.uniform(seeds[1], (NZ, NX, NY), jnp.float32) ** block_scale(seeds[1], (NZ, NX, NY), ((0, 8), (1, 16)), -0.2, 0.2), 0.2, 1.5),
        "sulfate": jnp.clip(0.2 + 1.3 * jax.random.uniform(seeds[2], (NZ, NX, NY), jnp.float32) ** block_scale(seeds[2], (NZ, NX, NY), ((0, 8), (1, 16)), -0.2, 0.2), 0.2, 1.5),
        "layer_of_cell": set_ends(jax.random.randint(seeds[3], (NZ,), 0, LAYERS), jax.random.fold_in(seeds[3], 1), 0, LAYERS - 1).astype(jnp.int32),
        "perm_horizontal": jnp.clip(jnp.exp(jax.random.uniform(seeds[4], (LAYERS,), jnp.float32, math.log(0.3), math.log(3.0))), 0.3, 3.0),
        "perm_vertical": jnp.clip(jnp.exp(jax.random.uniform(seeds[5], (LAYERS,), jnp.float32, math.log(0.3), math.log(3.0))), 0.3, 3.0),
        "vent_mask": set_ends((jax.random.randint(seeds[6], (NX, NY), 0, 16) < 1).astype(jnp.int32), jax.random.fold_in(seeds[6], 1), 0, 1),
    }


STORAGE = 0.004
COURANT = 0.5
REACTION = 4.0
VENT_INPUT = 4.0


def layer_tables(layer_of_cell, perm_horizontal, perm_vertical):
    levels = jnp.arange(perm_horizontal.shape[0], dtype=jnp.int32)
    picked = (layer_of_cell[:, None] == levels[None, :]).astype(jnp.float32)
    horizontal = jnp.sum(picked * perm_horizontal[None, :], axis=1)
    vertical = jnp.sum(picked * perm_vertical[None, :], axis=1)
    interior = 2.0 * vertical[:-1] * vertical[1:] / (vertical[:-1] + vertical[1:])
    boundary = jnp.zeros((1,), jnp.float32)
    return horizontal, jnp.concatenate([boundary, interior, boundary])


def eigen_values(number, offset, period):
    wave_index = (offset + jnp.arange(number, dtype=jnp.int32)) % period
    return 2.0 - 2.0 * jnp.cos(wave_index.astype(jnp.float32) * (2.0 * math.pi / period))


def eliminate(upper_face, lower_face, perm_column, spectrum, f_real, f_imag, initial):
    def advance(state_now, inputs):
        ratio_now, real_now, imag_now = state_now
        up_face, down_face, perm_value, source_real, source_imag = inputs
        pivot = (up_face + down_face + perm_value * spectrum + STORAGE) - up_face * ratio_now
        ratio_now = down_face / pivot
        real_now = (source_real + up_face * real_now) / pivot
        imag_now = (source_imag + up_face * imag_now) / pivot
        return (ratio_now, real_now, imag_now), (ratio_now, real_now, imag_now)
    return lax.scan(advance, initial, (upper_face, lower_face, perm_column, f_real, f_imag))


def substitute(ratios, h_real, h_imag, initial):
    def advance(state_now, inputs):
        real_now, imag_now = state_now
        ratio_now, head_real, head_imag = inputs
        real_now = head_real + ratio_now * real_now
        imag_now = head_imag + ratio_now * imag_now
        return (real_now, imag_now), (real_now, imag_now)
    _, solved = lax.scan(advance, initial, (ratios, h_real, h_imag), reverse=True)
    return solved


def upwind_divergence(concentration, east_face, north_face, vertical_face):
    flux_x = jnp.maximum(east_face, 0.0) * concentration + jnp.minimum(east_face, 0.0) * jnp.roll(concentration, -1, 1)
    flux_y = jnp.maximum(north_face, 0.0) * concentration + jnp.minimum(north_face, 0.0) * jnp.roll(concentration, -1, 2)
    padded = jnp.pad(concentration, ((1, 1), (0, 0), (0, 0)))
    flux_z = jnp.maximum(vertical_face, 0.0) * padded[:-1] + jnp.minimum(vertical_face, 0.0) * padded[1:]
    return (flux_x - jnp.roll(flux_x, 1, 1)) + (flux_y - jnp.roll(flux_y, 1, 2)) + (flux_z[1:] - flux_z[:-1])


def reference(source_field, methane, sulfate, layer_of_cell, perm_horizontal, perm_vertical, vent_mask):
    horizontal, face_coupling = layer_tables(layer_of_cell, perm_horizontal, perm_vertical)
    transformed = jnp.fft.fft2(source_field, axes=(1, 2))
    spectrum = eigen_values(NX, 0, NX)[:, None] + eigen_values(NY, 0, NY)[None, :]
    zeros_block = jnp.zeros((NX, NY), jnp.float32)
    _, (ratios, h_real, h_imag) = eliminate(face_coupling[:-1], face_coupling[1:], horizontal, spectrum,
                                            jnp.real(transformed), jnp.imag(transformed),
                                            (zeros_block, zeros_block, zeros_block))
    sol_real, sol_imag = substitute(ratios, h_real, h_imag, (zeros_block, zeros_block))
    pressure = jnp.real(jnp.fft.ifft2(sol_real + 1j * sol_imag, axes=(1, 2)))
    perm_column = horizontal[:, None, None]
    east_face = -perm_column * (jnp.roll(pressure, -1, 1) - pressure)
    north_face = -perm_column * (jnp.roll(pressure, -1, 2) - pressure)
    padded = jnp.pad(pressure, ((1, 1), (0, 0), (0, 0)))
    vertical_face = -face_coupling[:, None, None] * (padded[1:] - padded[:-1])
    face_speed = (jnp.abs(east_face) + jnp.abs(jnp.roll(east_face, 1, 1)) + jnp.abs(north_face)
                  + jnp.abs(jnp.roll(north_face, 1, 2)) + jnp.abs(vertical_face[:-1]) + jnp.abs(vertical_face[1:]))
    step_size = COURANT / (jnp.max(face_speed) + 1e-6)
    vent_field = vent_mask.astype(jnp.float32)[None]
    for sweep_index in range(STEPS):
        change_methane = upwind_divergence(methane, east_face, north_face, vertical_face)
        change_sulfate = upwind_divergence(sulfate, east_face, north_face, vertical_face)
        reaction = REACTION * methane * sulfate
        methane_next = methane - step_size * change_methane + step_size * (VENT_INPUT * vent_field - reaction)
        sulfate = sulfate - step_size * change_sulfate - step_size * reaction
        methane = methane_next
    return pressure, methane, sulfate
```

```python
import functools

import jax
import jax.numpy as jnp
import ml_dtypes
import numpy as np
from jax import lax
from jax.experimental import pallas as pl
from jax.experimental.pallas import tpu as pltpu
from jax.sharding import PartitionSpec as P

STEPS = 4
STORAGE = 0.004
COURANT = 0.5
REACTION = 4.0
VENT_INPUT = 4.0

NZ = 64
N = 512
NH = 16
ND = 8
ZL = 8
XL = 32
HALO = 4
ZE = ZL + 2 * HALO
XE = XL + 16
NB = NZ // 2

F32 = jnp.float32
BF16 = jnp.bfloat16


def tables():
    k = np.arange(N)
    angle = (k[:, None] * k[None, :] % N) * (2.0 * np.pi / N)
    cas = np.cos(angle) + np.sin(angle)
    hi = cas.astype(np.float32).astype(ml_dtypes.bfloat16)
    lo = (cas - hi.astype(np.float64)).astype(np.float32).astype(ml_dtypes.bfloat16)
    eig = (4.0 * np.sin(np.pi * k / N) ** 2).astype(np.float32)
    eig_x = np.broadcast_to(eig.reshape(NB, 16, 1), (NB, 16, 128)).copy()
    eig_y = np.broadcast_to(eig.reshape(4, 1, 128), (4, 16, 128)).copy()
    return hi, lo, eig_x, eig_y


def split(v):
    hi = v.astype(BF16)
    return hi, (v - hi.astype(F32)).astype(BF16)


def dot3(a, b):
    (ah, al), (bh, bl) = a, b
    d = functools.partial(jnp.dot, preferred_element_type=F32)
    return d(ah, bh) + (d(al, bh) + d(ah, bl))


def kernel(
    src, met, sul, layer, ph, pv, vent, hhi, hlo, eig_x, eig_y,
    out_p, out_m, out_s,
    y1, r1, zb, cb, r3, xb, y4,
    inv, ci, rat,
    ep, em, es, em2, es2, ev, pack, xin, coef, tend,
    mx, mxh, mxd, cpl, khs,
    s1, q1, s2, q2, s3, q3, s4, q4, hs, hq, vs, vq, ms, mq, ns, nq, lsem,
):
    h = lax.axis_index("horiz")
    d = lax.axis_index("depth")
    qb = lax.div(h, 4)
    qa = lax.rem(h, 4)
    b = d * 4 + qb

    def dev(hh, dd):
        return {"horiz": hh, "depth": dd}

    def mate(j):
        return lax.rem(h + j, NH)

    def fellow(j):
        pb = lax.rem(b + j, NB)
        return pb, lax.rem(pb, 4) * 4 + qa, lax.div(pb, 4)

    h_up, h_dn = lax.rem(h + 1, NH), lax.rem(h + NH - 1, NH)
    d_up, d_dn = lax.rem(d + 1, ND), lax.rem(d + ND - 1, ND)

    own_copies = [
        pltpu.make_async_copy(met, em.at[pl.ds(HALO, ZL), pl.ds(8, XL)], lsem.at[0]),
        pltpu.make_async_copy(sul, es.at[pl.ds(HALO, ZL), pl.ds(8, XL)], lsem.at[1]),
    ]
    for c in own_copies:
        c.start()

    barrier = pltpu.get_barrier_semaphore()

    def greet_h(j, _):
        pl.semaphore_signal(barrier, inc=1, device_id=dev(mate(j), d))
        return 0

    def greet_b(j, _):
        _, fh, fd = fellow(j)
        pl.semaphore_signal(barrier, inc=1, device_id=dev(fh, fd))
        return 0

    lax.fori_loop(1, NH, greet_h, 0)
    lax.fori_loop(1, NB, greet_b, 0)
    for hh in (h_up, h_dn):
        for dd in (d_up, d_dn):
            pl.semaphore_signal(barrier, inc=1, device_id=dev(hh, dd))

    def table(z, _):
        khs[z] = ph[layer[z]]
        return 0

    lax.fori_loop(0, NZ, table, 0)
    cpl[0] = 0.0
    cpl[NZ] = 0.0

    def face(i, _):
        a, c = pv[layer[i - 1]], pv[layer[i]]
        cpl[i] = 2.0 * a * c / (a + c)
        return 0

    lax.fori_loop(1, NZ, face, 0)

    hh_, hl_ = hhi[...], hlo[...]
    table_h = (hh_, hl_)
    s = split(src[...].reshape(ZL * XL, N))
    for n in range(2):
        cols = (hhi[:, 256 * n:256 * n + 256], hlo[:, 256 * n:256 * n + 256])
        o = dot3(s, cols)
        y1[2 * n] = o[:, :128].reshape(ZL, XL, 128)
        y1[2 * n + 1] = o[:, 128:].reshape(ZL, XL, 128)

    pl.semaphore_wait(barrier, (NH - 1) + (NB - 1) + 4)

    def copy1(j, origin):
        peer = mate(j)
        return pltpu.make_async_remote_copy(
            src_ref=y1.at[lax.rem(peer, 4), pl.ds(2 * lax.div(peer, 4), 2)],
            dst_ref=r1.at[:, pl.ds(pl.multiple_of(XL * origin, XL), XL), :],
            send_sem=s1.at[j], recv_sem=q1.at[j], device_id=dev(peer, d))

    def go1(j, _):
        copy1(j, h).start()
        return 0

    lax.fori_loop(1, NH, go1, 0)

    def halo_copies(f, ref, dirs):
        own = pl.ds(8, XL)
        lo_p, hi_p = pack.at[f, 0], pack.at[f, 1]
        plan = (
            (ref.at[pl.ds(8, 4), own], ref.at[pl.ds(0, 4), own], h, d_up),
            (ref.at[pl.ds(4, 4), own], ref.at[pl.ds(12, 4), own], h, d_dn),
            (hi_p, xin.at[f, 0, pl.ds(2, 4)], h_up, d),
            (lo_p, xin.at[f, 1, pl.ds(2, 4)], h_dn, d),
            (hi_p.at[pl.ds(2, 2)], xin.at[f, 0, pl.ds(0, 2)], h_up, d_up),
            (hi_p.at[pl.ds(0, 2)], xin.at[f, 0, pl.ds(6, 2)], h_up, d_dn),
            (lo_p.at[pl.ds(2, 2)], xin.at[f, 1, pl.ds(0, 2)], h_dn, d_up),
            (lo_p.at[pl.ds(0, 2)], xin.at[f, 1, pl.ds(6, 2)], h_dn, d_dn),
        )
        return [
            pltpu.make_async_remote_copy(
                src_ref=plan[i][0], dst_ref=plan[i][1], send_sem=hs.at[f, i], recv_sem=hq.at[f, i],
                device_id=dev(plan[i][2], plan[i][3]))
            for i in dirs
        ]

    sub8 = lax.broadcasted_iota(jnp.int32, (8, N), 0)

    def pack_rows(f, ref):
        for zz in range(ZL // 2):
            even, odd = ref[HALO + 2 * zz], ref[HALO + 2 * zz + 1]
            pack[f, 0, zz] = jnp.where(sub8 < 4, even[8:16], pltpu.roll(odd[8:16], 4, 0))
            pack[f, 1, zz] = jnp.where(sub8 >= 4, even[32:40], pltpu.roll(odd[32:40], 4, 0))

    def unpack_rows(f, ref):
        for zz in range(ZE // 2):
            for side, row in ((0, 0), (1, 40)):
                tile = xin[f, side, zz]
                ref[2 * zz, row:row + 8] = tile
                ref[2 * zz + 1, row:row + 8] = pltpu.roll(tile, 4, 0)

    for c in own_copies:
        c.wait()
    conc = ((1, em), (2, es))
    for f, ref in conc:
        for c in halo_copies(f, ref, (0, 1)):
            c.start()
    for f, ref in conc:
        pack_rows(f, ref)
    ev[8:40] = vent[...].astype(F32)
    vent_copies = [
        pltpu.make_async_remote_copy(
            src_ref=ev.at[pl.ds(32, 8)], dst_ref=ev.at[pl.ds(0, 8)],
            send_sem=vs.at[0], recv_sem=vq.at[0], device_id=dev(h_up, d)),
        pltpu.make_async_remote_copy(
            src_ref=ev.at[pl.ds(8, 8)], dst_ref=ev.at[pl.ds(40, 8)],
            send_sem=vs.at[1], recv_sem=vq.at[1], device_id=dev(h_dn, d)),
    ]

    lam = eig_x[b] + eig_y[qa]

    def factor(z, r):
        cu, cd = cpl[z], cpl[z + 1]
        den = (cu + cd + khs[z] * lam + STORAGE) - cu * r
        i = 1.0 / den
        r = cd * i
        inv[z] = i
        ci[z] = cu * i
        rat[z] = r
        return r

    lax.fori_loop(0, NZ, factor, jnp.zeros((16, 128), F32))

    own_x = pl.ds(pl.multiple_of(XL * h, XL), XL)
    r1[:, own_x, :] = y1[qa, pl.ds(2 * qb, 2)]

    def done1(j, _):
        copy1(j, lax.rem(h + NH - j, NH)).wait_recv()
        return 0

    lax.fori_loop(1, NH, done1, 0)

    o = dot3(table_h, split(jnp.concatenate([r1[0], r1[1]], axis=1)))
    zb[0] = o[:, :128]
    zb[1] = o[:, 128:]

    def copy2(j, origin):
        pb, fh, fd = fellow(j)
        return pltpu.make_async_remote_copy(
            src_ref=zb.at[:, pl.ds(pl.multiple_of(16 * pb, 16), 16), :],
            dst_ref=cb.at[pl.ds(2 * origin, 2)],
            send_sem=s2.at[j], recv_sem=q2.at[j], device_id=dev(fh, fd))

    def go2(j, _):
        copy2(j, b).start()
        return 0

    lax.fori_loop(1, NB, go2, 0)
    for f, ref in conc:
        for c in halo_copies(f, ref, range(2, 8)):
            c.start()
    for c in vent_copies:
        c.start()
    own_k = pl.ds(pl.multiple_of(16 * b, 16), 16)
    cb[pl.ds(2 * b, 2)] = zb[:, own_k, :]

    def done2(j, _):
        copy2(j, lax.rem(b + NB - j, NB)).wait_recv()
        return 0

    lax.fori_loop(1, NB, done2, 0)

    def down(z, hz):
        hz = cb[z] * (inv[z] * (1.0 / (N * N))) + ci[z] * hz
        cb[z] = hz
        return hz

    lax.fori_loop(0, NZ, down, jnp.zeros((16, 128), F32), unroll=8)

    def up(i, p):
        z = NZ - 1 - i
        p = cb[z] + rat[z] * p
        cb[z] = p
        return p

    lax.fori_loop(0, NZ, up, jnp.zeros((16, 128), F32), unroll=8)

    def copy3(j, origin):
        pb, fh, fd = fellow(j)
        return pltpu.make_async_remote_copy(
            src_ref=cb.at[pl.ds(2 * pb, 2)],
            dst_ref=r3.at[:, pl.ds(pl.multiple_of(16 * origin, 16), 16), :],
            send_sem=s3.at[j], recv_sem=q3.at[j], device_id=dev(fh, fd))

    def go3(j, _):
        copy3(j, b).start()
        return 0

    lax.fori_loop(1, NB, go3, 0)
    r3[:, own_k, :] = cb[pl.ds(2 * b, 2)]

    def done3(j, _):
        copy3(j, lax.rem(b + NB - j, NB)).wait_recv()
        return 0

    lax.fori_loop(1, NB, done3, 0)

    o = dot3(table_h, split(jnp.concatenate([r3[0], r3[1]], axis=1)))
    xb[0] = o[:, :128]
    xb[1] = o[:, 128:]

    def copy4(j, oa, ob):
        peer = mate(j)
        return pltpu.make_async_remote_copy(
            src_ref=xb.at[:, pl.ds(pl.multiple_of(XL * peer, XL), XL), :],
            dst_ref=y4.at[oa, pl.ds(2 * ob, 2)],
            send_sem=s4.at[j], recv_sem=q4.at[j], device_id=dev(peer, d))

    def go4(j, _):
        copy4(j, qa, qb).start()
        return 0

    lax.fori_loop(1, NH, go4, 0)
    y4[qa, pl.ds(2 * qb, 2)] = xb[:, own_x, :]

    for f, ref in conc:
        for c in halo_copies(f, ref, range(8)):
            c.wait()
        unpack_rows(f, ref)
    for c in vent_copies:
        c.wait()

    def done4(j, _):
        origin = lax.rem(h + NH - j, NH)
        copy4(j, lax.rem(origin, 4), lax.div(origin, 4)).wait_recv()
        return 0

    lax.fori_loop(1, NH, done4, 0)

    s = split(jnp.concatenate([y4[k].reshape(ZL * XL, 128) for k in range(4)], axis=1))
    for n in range(2):
        o = dot3(s, (hhi[:, 256 * n:256 * n + 256], hlo[:, 256 * n:256 * n + 256]))
        ep[HALO:HALO + ZL, 8:40, 256 * n:256 * n + 256] = o.reshape(ZL, XL, 256)
    out_p[...] = ep[HALO:HALO + ZL, 8:40, :]

    pack_rows(0, ep)
    p_halo = halo_copies(0, ep, range(8))
    for c in p_halo:
        c.start()
    for c in p_halo:
        c.wait_recv()
    unpack_rows(0, ep)

    def cell(i):
        gz = lax.rem(d * ZL + i + (NZ - HALO), NZ)
        kh, cu, cd = khs[gz], cpl[gz], cpl[gz + 1]
        p = ep[i]
        east = -kh * (pltpu.roll(p, XE - 1, 0) - p)
        north = -kh * (pltpu.roll(p, N - 1, 1) - p)
        above = -cu * (p - ep[i - 1])
        below = -cd * (ep[i + 1] - p)
        return east, pltpu.roll(east, 1, 0), north, pltpu.roll(north, 1, 1), above, below

    def speed(i, m):
        e, w, n, s_, a, c = [jnp.abs(v[8:40]) for v in cell(i)]
        v = e + w + n + s_ + a + c
        v = jnp.max(v.reshape(4, 8, N), axis=0)
        return jnp.maximum(m, jnp.maximum(jnp.maximum(v[:, :128], v[:, 128:256]),
                                          jnp.maximum(v[:, 256:384], v[:, 384:])))

    mx[0] = lax.fori_loop(HALO, HALO + ZL, speed, jnp.zeros((8, 128), F32))

    def copy_m(j, origin):
        return pltpu.make_async_remote_copy(
            src_ref=mx.at[0], dst_ref=mxh.at[origin], send_sem=ms.at[j], recv_sem=mq.at[j],
            device_id=dev(mate(j), d))

    def copy_n(j, origin):
        return pltpu.make_async_remote_copy(
            src_ref=mx.at[1], dst_ref=mxd.at[origin], send_sem=ns.at[j], recv_sem=nq.at[j],
            device_id=dev(h, lax.rem(d + j, ND)))

    def go_m(j, _):
        copy_m(j, h).start()
        return 0

    lax.fori_loop(1, NH, go_m, 0)
    mxh[h] = mx[0]

    def stencil(get, c_ref, i):
        c = c_ref[i]
        return (get(0) * c
                + get(1) * pltpu.roll(c, XE - 1, 0) + get(2) * pltpu.roll(c, 1, 0)
                + get(3) * pltpu.roll(c, N - 1, 1) + get(4) * pltpu.roll(c, 1, 1)
                + get(5) * c_ref[i + 1] + get(6) * c_ref[i - 1])

    def tendencies(m_ref, s_ref, i):
        get = lambda k: coef[k, i - 1]
        react = REACTION * m_ref[i] * s_ref[i]
        return (stencil(get, m_ref, i) + (react - VENT_INPUT * ev[...]),
                stencil(get, s_ref, i) + react)

    def prepare(i, _):
        e, w, n, s_, a, c = cell(i)
        pos, neg = (lambda v: jnp.maximum(v, 0.0)), (lambda v: jnp.minimum(v, 0.0))
        coef[0, i - 1] = (pos(e) - neg(w)) + (pos(n) - neg(s_)) + (pos(c) - neg(a))
        coef[1, i - 1] = neg(e)
        coef[2, i - 1] = -pos(w)
        coef[3, i - 1] = neg(n)
        coef[4, i - 1] = -pos(s_)
        coef[5, i - 1] = neg(c)
        coef[6, i - 1] = -pos(a)
        t_m, t_s = tendencies(em, es, i)
        tend[0, i - 1] = t_m
        tend[1, i - 1] = t_s
        return 0

    lax.fori_loop(1, 8, prepare, 0)

    def done_m(j, _):
        copy_m(j, lax.rem(h + NH - j, NH)).wait_recv()
        return 0

    lax.fori_loop(1, NH, done_m, 0)
    mx[1] = jnp.max(mxh[...], axis=0)

    def go_n(j, _):
        copy_n(j, d).start()
        return 0

    lax.fori_loop(1, ND, go_n, 0)
    mxd[d] = mx[1]

    lax.fori_loop(8, ZE - 1, prepare, 0)

    def done_n(j, _):
        copy_n(j, lax.rem(d + ND - j, ND)).wait_recv()
        return 0

    lax.fori_loop(1, ND, done_n, 0)
    fastest = jnp.max(jnp.max(mxd[...], axis=0), axis=(0, 1), keepdims=True)
    dt = COURANT / (fastest + 1e-6)

    def first(i, _):
        em2[i] = em[i] - dt * tend[0, i - 1]
        es2[i] = es[i] - dt * tend[1, i - 1]
        return 0

    lax.fori_loop(1, ZE - 1, first, 0)

    def step(a, c, lo):
        def body(i, _):
            t_m, t_s = tendencies(a[0], a[1], i)
            c[0][i] = a[0][i] - dt * t_m
            c[1][i] = a[1][i] - dt * t_s
            return 0

        lax.fori_loop(lo, ZE - lo, body, 0)

    step((em2, es2), (em, es), 2)
    step((em, es), (em2, es2), 3)

    def last(i, _):
        t_m, t_s = tendencies(em2, es2, i)
        out_m[i - HALO] = (em2[i] - dt * t_m)[8:40]
        out_s[i - HALO] = (es2[i] - dt * t_s)[8:40]
        return 0

    lax.fori_loop(HALO, HALO + ZL, last, 0)

    def left_h(j, _):
        copy1(j, h).wait_send()
        copy4(j, qa, qb).wait_send()
        copy_m(j, h).wait_send()
        return 0

    def left_b(j, _):
        copy2(j, b).wait_send()
        copy3(j, b).wait_send()
        return 0

    def left_d(j, _):
        copy_n(j, d).wait_send()
        return 0

    lax.fori_loop(1, NH, left_h, 0)
    lax.fori_loop(1, NB, left_b, 0)
    lax.fori_loop(1, ND, left_d, 0)
    for c in p_halo:
        c.wait_send()


def local(source_field, methane, sulfate, layer_of_cell, perm_horizontal, perm_vertical, vent_mask):
    hi, lo, eig_x, eig_y = tables()
    vmem = pl.BlockSpec(memory_space=pltpu.VMEM)
    smem = pl.BlockSpec(memory_space=pltpu.SMEM)
    hbm = pl.BlockSpec(memory_space=pl.ANY)
    field = jax.ShapeDtypeStruct((ZL, XL, N), F32)
    dma = pltpu.SemaphoreType.DMA
    ext = pltpu.VMEM((ZE, XE, N), F32)
    scratch = [
        pltpu.VMEM((4, ZL, XL, 128), F32),
        pltpu.VMEM((2, N, 128), F32),
        pltpu.VMEM((2, N, 128), F32),
        pltpu.VMEM((NZ, 16, 128), F32),
        pltpu.VMEM((2, N, 128), F32),
        pltpu.VMEM((2, N, 128), F32),
        pltpu.VMEM((4, ZL, XL, 128), F32),
        pltpu.VMEM((NZ, 16, 128), F32),
        pltpu.VMEM((NZ, 16, 128), F32),
        pltpu.VMEM((NZ, 16, 128), F32),
        ext, ext, ext, ext, ext,
        pltpu.VMEM((XE, N), F32),
        pltpu.VMEM((3, 2, ZL // 2, 8, N), F32),
        pltpu.VMEM((3, 2, ZE // 2, 8, N), F32),
        pltpu.VMEM((7, ZE - 2, XE, N), F32),
        pltpu.VMEM((2, ZE - 2, XE, N), F32),
        pltpu.VMEM((2, 8, 128), F32),
        pltpu.VMEM((NH, 8, 128), F32),
        pltpu.VMEM((ND, 8, 128), F32),
        pltpu.SMEM((NZ + 1,), F32),
        pltpu.SMEM((NZ,), F32),
        dma((NH,)), dma((NH,)), dma((NB,)), dma((NB,)), dma((NB,)), dma((NB,)), dma((NH,)), dma((NH,)),
        dma((3, 8)), dma((3, 8)), dma((2,)), dma((2,)),
        dma((NH,)), dma((NH,)), dma((ND,)), dma((ND,)), dma((2,)),
    ]
    return pl.pallas_call(
        kernel,
        out_shape=(field, field, field),
        in_specs=[vmem, hbm, hbm, smem, smem, smem, vmem, vmem, vmem, vmem, vmem],
        out_specs=(vmem, vmem, vmem),
        scratch_shapes=scratch,
        compiler_params=pltpu.CompilerParams(
            collective_id=0, has_side_effects=True, vmem_limit_bytes=60 * 1024 * 1024),
    )(source_field, methane, sulfate, layer_of_cell, perm_horizontal, perm_vertical, vent_mask,
      jnp.asarray(hi), jnp.asarray(lo), jnp.asarray(eig_x), jnp.asarray(eig_y))


def solution(mesh):
    field = P("depth", "horiz", None)
    return jax.shard_map(
        local,
        mesh=mesh,
        in_specs=(field, field, field, P(), P(), P(), P("horiz", None)),
        out_specs=(field, field, field),
        check_vma=False,
    )
```

```python
import jax
import jax.numpy as jnp
import ml_dtypes
import numpy as np
from jax import lax
from jax.experimental import pallas as pl
from jax.experimental.pallas import tpu as pltpu
from jax.sharding import PartitionSpec as P

STEPS = 4
STORAGE = 0.004
COURANT = 0.5
REACTION = 4.0
VENT_INPUT = 4.0

NZ = 64
N = 512
NH = 16
ND = 8
ZL = 8
XL = 32
HALO = 4
ZE = ZL + 2 * HALO
XE = XL + 16
NX_CHIPS = 4
ZB = NZ // NX_CHIPS
NQ = 2 * NH

F32 = jnp.float32
BF16 = jnp.bfloat16


def tables():
    k = np.arange(N)
    angle = (k[:, None] * k[None, :] % N) * (2.0 * np.pi / N)
    cas = np.cos(angle) + np.sin(angle)
    hi = cas.astype(np.float32).astype(ml_dtypes.bfloat16)
    lo = (cas - hi.astype(np.float64)).astype(np.float32).astype(ml_dtypes.bfloat16)
    eig = (4.0 * np.sin(np.pi * k / N) ** 2).astype(np.float32)
    eig_x = np.broadcast_to(eig.reshape(1, N), (16, N)).copy()
    eig_y = np.broadcast_to(eig.reshape(NQ, 16, 1), (NQ, 16, 128)).copy()
    return hi, lo, eig_x, eig_y


def split(v):
    hi = v.astype(BF16)
    return hi, (v - hi.astype(F32)).astype(BF16)


def dot3(a, b, dims=((1,), (0,))):
    (ah, al), (bh, bl) = a, b
    d = lambda x, y: lax.dot_general(x, y, (dims, ((), ())), preferred_element_type=F32)
    return d(ah, bh) + (d(al, bh) + d(ah, bl))


def kernel(
    src, met, sul, layer, ph, pv, vent, hhi, hlo, eig_x, eig_y,
    out_p, out_m, out_s,
    y1, r1, ah, al, fz, w1, y4, ey,
    inv_d, inv_u, prod_d, prod_u, gd, pi, send_a, recv_a,
    ep, em, es, em2, es2, ev, pack, xin, coef, tend,
    mx, mxh, mxd, cpl, khs,
    s1, q1, s2, q2, s4, q4, hs, hq, vs, vq, ms, mq, ns, nq, lsem,
):
    h = lax.axis_index("horiz")
    d = lax.axis_index("depth")
    chip = lax.div(d, 2)
    core = lax.rem(d, 2)
    q = h * 2 + core

    drains = {}

    def dev(hh, dd):
        return {"horiz": hh, "depth": dd}

    def mate(j):
        return lax.rem(h + j, NH)

    def fellow(j):
        pq = lax.rem(q + j, NQ)
        return pq, lax.div(pq, 2), lax.rem(pq, 2)

    def slot(oq):
        return lax.rem(oq, 2) * NH + lax.div(oq, 2)

    h_up, h_dn = lax.rem(h + 1, NH), lax.rem(h + NH - 1, NH)
    d_up, d_dn = lax.rem(d + 1, ND), lax.rem(d + ND - 1, ND)

    barrier = pltpu.get_barrier_semaphore()

    def greet_q(j, _):
        _, fh, fc = fellow(j)
        pl.semaphore_signal(barrier, inc=1, device_id=dev(fh, 2 * chip + fc))
        return 0

    def greet_d(j, _):
        pl.semaphore_signal(barrier, inc=1, device_id=dev(h, lax.rem(d + j, ND)))
        return 0

    lax.fori_loop(1, NQ, greet_q, 0)
    lax.fori_loop(1, ND, greet_d, 0)
    for hh in (h_up, h_dn):
        for dd in (d_up, d_dn):
            pl.semaphore_signal(barrier, inc=1, device_id=dev(hh, dd))

    own_copies = [
        pltpu.make_async_copy(met, em.at[pl.ds(HALO, ZL), pl.ds(8, XL)], lsem.at[0]),
        pltpu.make_async_copy(sul, es.at[pl.ds(HALO, ZL), pl.ds(8, XL)], lsem.at[1]),
    ]
    own_copies.append(pltpu.make_async_copy(eig_y.at[q], ey, lsem.at[2]))
    for c in own_copies:
        c.start()
    drains["own"] = lambda: [c.wait() for c in own_copies]

    s = split(src[...].reshape(ZL * XL, N))
    for n in range(2):
        rows = (hhi[256 * n:256 * n + 256], hlo[256 * n:256 * n + 256])
        y1[16 * n:16 * n + 16] = dot3(rows, s, ((1,), (1,))).reshape(16, 16, ZL * XL)

    pl.semaphore_wait(barrier, (NQ - 1) + (ND - 1) + 4)

    def copy1(j, oq):
        pq, fh, fc = fellow(j)
        return pltpu.make_async_remote_copy(
            src_ref=y1.at[pq], dst_ref=r1.at[slot(oq)],
            send_sem=s1.at[j], recv_sem=q1.at[j], device_id=dev(fh, 2 * chip + fc))

    def go1(j, _):
        copy1(j, q).start()
        return 0

    lax.fori_loop(1, NQ, go1, 0)
    def left1(j, _):
        copy1(j, q).wait_send()
        return 0
    drains["1"] = lambda: lax.fori_loop(1, NQ, left1, 0)

    def halo_copies(f, ref, dirs):
        own = pl.ds(8, XL)
        lo_p, hi_p = pack.at[f, 0], pack.at[f, 1]
        plan = (
            (ref.at[pl.ds(8, 4), own], ref.at[pl.ds(0, 4), own], h, d_up),
            (ref.at[pl.ds(4, 4), own], ref.at[pl.ds(12, 4), own], h, d_dn),
            (hi_p, xin.at[f, 0, pl.ds(2, 4)], h_up, d),
            (lo_p, xin.at[f, 1, pl.ds(2, 4)], h_dn, d),
            (hi_p.at[pl.ds(2, 2)], xin.at[f, 0, pl.ds(0, 2)], h_up, d_up),
            (hi_p.at[pl.ds(0, 2)], xin.at[f, 0, pl.ds(6, 2)], h_up, d_dn),
            (lo_p.at[pl.ds(2, 2)], xin.at[f, 1, pl.ds(0, 2)], h_dn, d_up),
            (lo_p.at[pl.ds(0, 2)], xin.at[f, 1, pl.ds(6, 2)], h_dn, d_dn),
        )
        return [
            pltpu.make_async_remote_copy(
                src_ref=plan[i][0], dst_ref=plan[i][1], send_sem=hs.at[f, i], recv_sem=hq.at[f, i],
                device_id=dev(plan[i][2], plan[i][3]))
            for i in dirs
        ]

    sub8 = lax.broadcasted_iota(jnp.int32, (8, N), 0)

    def pack_rows(f, ref):
        for zz in range(ZL // 2):
            even, odd = ref[HALO + 2 * zz], ref[HALO + 2 * zz + 1]
            pack[f, 0, zz] = jnp.where(sub8 < 4, even[8:16], pltpu.roll(odd[8:16], 4, 0))
            pack[f, 1, zz] = jnp.where(sub8 >= 4, even[32:40], pltpu.roll(odd[32:40], 4, 0))

    def unpack_rows(f, ref):
        for zz in range(ZE // 2):
            for side, row in ((0, 0), (1, 40)):
                tile = xin[f, side, zz]
                ref[2 * zz, row:row + 8] = tile
                ref[2 * zz + 1, row:row + 8] = pltpu.roll(tile, 4, 0)

    def table(z, _):
        khs[z] = ph[layer[z]]
        return 0

    lax.fori_loop(0, NZ, table, 0)
    cpl[0] = 0.0
    cpl[NZ] = 0.0

    def face(i, _):
        a, c = pv[layer[i - 1]], pv[layer[i]]
        cpl[i] = 2.0 * a * c / (a + c)
        return 0

    lax.fori_loop(1, NZ, face, 0)

    drains.pop("own")()
    conc = ((1, em), (2, es))
    for f, ref in conc:
        for c in halo_copies(f, ref, (0, 1)):
            c.start()
    drains["c01"] = lambda: [c.wait() for f, ref in conc for c in halo_copies(f, ref, (0, 1))]
    for f, ref in conc:
        pack_rows(f, ref)
    ev[8:40] = vent[...].astype(F32)
    vent_copies = [
        pltpu.make_async_remote_copy(
            src_ref=ev.at[pl.ds(32, 8)], dst_ref=ev.at[pl.ds(0, 8)],
            send_sem=vs.at[0], recv_sem=vq.at[0], device_id=dev(h_up, d)),
        pltpu.make_async_remote_copy(
            src_ref=ev.at[pl.ds(8, 8)], dst_ref=ev.at[pl.ds(40, 8)],
            send_sem=vs.at[1], recv_sem=vq.at[1], device_id=dev(h_dn, d)),
    ]

    lam = eig_x[...] + jnp.concatenate([ey[...]] * 4, axis=1)
    blank = jnp.zeros((16, N), F32)
    state = (blank, blank)
    for j in range(NX_CHIPS):
        def factor(i, carry, j=j):
            rd, ru, bd, bu = carry
            z, y = ZB * j + i, NZ - 1 - ZB * j - i
            cu, cd = cpl[z], cpl[z + 1]
            v = 1.0 / ((cu + cd + khs[z] * lam + STORAGE) - cu * rd)
            inv_d[z] = v
            rd, bd = cd * v, bd * (cu * v)
            cu, cd = cpl[y], cpl[y + 1]
            v = 1.0 / ((cu + cd + khs[y] * lam + STORAGE) - cd * ru)
            inv_u[y] = v
            ru, bu = cu * v, bu * (cd * v)
            return rd, ru, bd, bu

        rd, ru, bd, bu = lax.fori_loop(0, ZB, factor, state + (blank + 1.0, blank + 1.0))
        state = (rd, ru)
        prod_d[j] = bd
        prod_u[NX_CHIPS - 1 - j] = bu
    base = ZB * chip

    def product(i, v):
        v = v * (cpl[base + i] * inv_d[base + i])
        pi[i] = v
        return v

    lax.fori_loop(0, ZB, product, blank + 1.0)
    r_last = cpl[base + ZB] * inv_d[base + ZB - 1]
    r_next = cpl[base + ZB] * inv_u[jnp.minimum(base + ZB, NZ - 1)]
    join = 1.0 / (1.0 - r_last * r_next)

    r1[slot(q)] = y1[q]

    def done1(j, _):
        copy1(j, lax.rem(q + NQ - j, NQ)).wait_recv()
        return 0

    lax.fori_loop(1, NQ, done1, 0)
    for f, ref in conc:
        for c in halo_copies(f, ref, range(2, 8)):
            c.start()
    for c in vent_copies:
        c.start()
    drains["c28"] = lambda: [c.wait() for c in vent_copies + [c for f, ref in conc for c in halo_copies(f, ref, range(2, 8))]]

    group = lax.broadcasted_iota(jnp.int32, (16, 128), 1) // 32

    def regroup(v):
        lower, even = group < 2, lax.rem(group, 2) == 0
        p = [jnp.where(lower, v[i], pltpu.roll(v[i + 2], 64, 1)) for i in range(2)]
        r = [jnp.where(lower, pltpu.roll(v[i], 64, 1), v[i + 2]) for i in range(2)]
        out = []
        for a, b in (p, r):
            out.append(jnp.where(even, a, pltpu.roll(b, 32, 1)))
            out.append(jnp.where(even, pltpu.roll(a, 96, 1), b))
        return out

    for c in range(2):
        for g in range(2):
            for t in range(4):
                v = regroup([r1[NH * c + 4 * t + i, :, 128 * g:128 * g + 128] for i in range(4)])
                for i in range(4):
                    row = 16 * (8 * c + 4 * g + i)
                    hi, lo = split(v[i])
                    ah[row:row + 16, 128 * t:128 * t + 128] = hi
                    al[row:row + 16, 128 * t:128 * t + 128] = lo
    for n in range(2):
        cols = (hhi[:, 256 * n:256 * n + 256], hlo[:, 256 * n:256 * n + 256])
        o = dot3((ah[...], al[...]), cols)
        fz[:, :, 256 * n:256 * n + 256] = (o * (1.0 / (N * N))).reshape(ZB, 16, 256)

    def down(i, v):
        k = inv_d[base + i]
        v = fz[i] * k + (cpl[base + i] * k) * v
        gd[i] = v
        return v

    def upward(n, v):
        i = ZB - 1 - n
        k = inv_u[base + i]
        return fz[i] * k + (cpl[base + i + 1] * k) * v

    send_a[0] = lax.fori_loop(0, ZB, down, blank, unroll=4)
    send_a[1] = lax.fori_loop(0, ZB, upward, blank, unroll=4)

    def copy2(j, origin):
        to = lax.rem(chip + j, NX_CHIPS)
        return pltpu.make_async_remote_copy(
            src_ref=send_a.at[jnp.where(to > chip, 0, 1)], dst_ref=recv_a.at[origin],
            send_sem=s2.at[j], recv_sem=q2.at[j], device_id=dev(h, 2 * to + core))

    def go2(j, _):
        copy2(j, chip).start()
        return 0

    lax.fori_loop(1, NX_CHIPS, go2, 0)

    def left2(j, _):
        copy2(j, chip).wait_send()
        return 0

    drains["2"] = lambda: lax.fori_loop(1, NX_CHIPS, left2, 0)
    recv_a[chip] = blank

    def done2(j, _):
        copy2(j, lax.rem(chip + NX_CHIPS - j, NX_CHIPS)).wait_recv()
        return 0

    lax.fori_loop(1, NX_CHIPS, done2, 0)
    from_top, from_bottom = blank, blank
    for j in range(NX_CHIPS - 1):
        from_top = jnp.where(j < chip, recv_a[j] + prod_d[j] * from_top, from_top)
        k = NX_CHIPS - 1 - j
        from_bottom = jnp.where(k > chip, recv_a[k] + prod_u[k] * from_bottom, from_bottom)

    def solved(i, p):
        row = pl.ds(pl.multiple_of(16 * i, 16), 16)
        hi, lo = split(p)
        ah[row, :] = hi
        al[row, :] = lo

    p = (gd[ZB - 1] + pi[ZB - 1] * from_top + r_last * from_bottom) * join
    solved(ZB - 1, p)

    def up(n, p):
        i = ZB - 2 - n
        p = gd[i] + pi[i] * from_top + (cpl[base + i + 1] * inv_d[base + i]) * p
        solved(i, p)
        return p

    lax.fori_loop(0, ZB - 1, up, p)
    for n in range(2):
        cols = (hhi[:, 256 * n:256 * n + 256], hlo[:, 256 * n:256 * n + 256])
        fz[:, :, 256 * n:256 * n + 256] = dot3((ah[...], al[...]), cols).reshape(ZB, 16, 256)
    for c in range(2):
        for g in range(2):
            for t in range(4):
                v = regroup([fz[8 * c + 4 * g + i, :, 128 * t:128 * t + 128] for i in range(4)])
                for i in range(4):
                    w1[NH * c + 4 * t + i, :, 128 * g:128 * g + 128] = v[i]

    def copy4(j, oq):
        pq, fh, fc = fellow(j)
        return pltpu.make_async_remote_copy(
            src_ref=w1.at[slot(pq)], dst_ref=y4.at[oq],
            send_sem=s4.at[j], recv_sem=q4.at[j], device_id=dev(fh, 2 * chip + fc))

    def go4(j, _):
        copy4(j, q).start()
        return 0

    lax.fori_loop(1, NQ, go4, 0)

    def left4(j, _):
        copy4(j, q).wait_send()
        return 0

    drains["4"] = lambda: lax.fori_loop(1, NQ, left4, 0)
    y4[q] = w1[slot(q)]

    del drains["c01"], drains["c28"]
    for f, ref in conc:
        for c in halo_copies(f, ref, range(8)):
            c.wait()
        unpack_rows(f, ref)
    for c in vent_copies:
        c.wait()

    def done4(j, _):
        copy4(j, lax.rem(q + NQ - j, NQ)).wait_recv()
        return 0

    lax.fori_loop(1, NQ, done4, 0)

    s = split(y4[...].reshape(N, ZL * XL).T)
    for n in range(2):
        o = dot3(s, (hhi[:, 256 * n:256 * n + 256], hlo[:, 256 * n:256 * n + 256]))
        ep[HALO:HALO + ZL, 8:40, 256 * n:256 * n + 256] = o.reshape(ZL, XL, 256)
    out_p[...] = ep[HALO:HALO + ZL, 8:40, :]

    pack_rows(0, ep)
    p_halo = halo_copies(0, ep, range(8))
    for c in p_halo:
        c.start()
    for c in p_halo:
        c.wait_recv()
    drains["p"] = lambda: [c.wait_send() for c in p_halo]
    unpack_rows(0, ep)

    def cell(i):
        gz = lax.rem(d * ZL + i + (NZ - HALO), NZ)
        kh, cu, cd = khs[gz], cpl[gz], cpl[gz + 1]
        p = ep[i]
        east = -kh * (pltpu.roll(p, XE - 1, 0) - p)
        north = -kh * (pltpu.roll(p, N - 1, 1) - p)
        above = -cu * (p - ep[i - 1])
        below = -cd * (ep[i + 1] - p)
        return east, pltpu.roll(east, 1, 0), north, pltpu.roll(north, 1, 1), above, below

    def speed(i, m):
        e, w, n, s_, a, c = [jnp.abs(v[8:40]) for v in cell(i)]
        v = e + w + n + s_ + a + c
        v = jnp.max(v.reshape(4, 8, N), axis=0)
        return jnp.maximum(m, jnp.maximum(jnp.maximum(v[:, :128], v[:, 128:256]),
                                          jnp.maximum(v[:, 256:384], v[:, 384:])))

    mx[0] = lax.fori_loop(HALO, HALO + ZL, speed, jnp.zeros((8, 128), F32))

    def copy_m(j, origin):
        return pltpu.make_async_remote_copy(
            src_ref=mx.at[0], dst_ref=mxh.at[origin], send_sem=ms.at[j], recv_sem=mq.at[j],
            device_id=dev(mate(j), d))

    def copy_n(j, origin):
        return pltpu.make_async_remote_copy(
            src_ref=mx.at[1], dst_ref=mxd.at[origin], send_sem=ns.at[j], recv_sem=nq.at[j],
            device_id=dev(h, lax.rem(d + j, ND)))

    def go_m(j, _):
        copy_m(j, h).start()
        return 0

    lax.fori_loop(1, NH, go_m, 0)
    def left_m(j, _):
        copy_m(j, h).wait_send()
        return 0
    drains["m"] = lambda: lax.fori_loop(1, NH, left_m, 0)
    mxh[h] = mx[0]

    def stencil(get, c_ref, i):
        c = c_ref[i]
        return (get(0) * c
                + get(1) * pltpu.roll(c, XE - 1, 0) + get(2) * pltpu.roll(c, 1, 0)
                + get(3) * pltpu.roll(c, N - 1, 1) + get(4) * pltpu.roll(c, 1, 1)
                + get(5) * c_ref[i + 1] + get(6) * c_ref[i - 1])

    def tendencies(m_ref, s_ref, i):
        get = lambda k: coef[k, i - 1]
        react = REACTION * m_ref[i] * s_ref[i]
        return (stencil(get, m_ref, i) + (react - VENT_INPUT * ev[...]),
                stencil(get, s_ref, i) + react)

    def prepare(i, _):
        e, w, n, s_, a, c = cell(i)
        pos, neg = (lambda v: jnp.maximum(v, 0.0)), (lambda v: jnp.minimum(v, 0.0))
        coef[0, i - 1] = (pos(e) - neg(w)) + (pos(n) - neg(s_)) + (pos(c) - neg(a))
        coef[1, i - 1] = neg(e)
        coef[2, i - 1] = -pos(w)
        coef[3, i - 1] = neg(n)
        coef[4, i - 1] = -pos(s_)
        coef[5, i - 1] = neg(c)
        coef[6, i - 1] = -pos(a)
        t_m, t_s = tendencies(em, es, i)
        tend[0, i - 1] = t_m
        tend[1, i - 1] = t_s
        return 0

    lax.fori_loop(1, 8, prepare, 0)

    def done_m(j, _):
        copy_m(j, lax.rem(h + NH - j, NH)).wait_recv()
        return 0

    lax.fori_loop(1, NH, done_m, 0)
    mx[1] = jnp.max(mxh[...], axis=0)

    def go_n(j, _):
        copy_n(j, d).start()
        return 0

    lax.fori_loop(1, ND, go_n, 0)
    def left_n(j, _):
        copy_n(j, d).wait_send()
        return 0
    drains["n"] = lambda: lax.fori_loop(1, ND, left_n, 0)
    mxd[d] = mx[1]

    lax.fori_loop(8, ZE - 1, prepare, 0)

    def done_n(j, _):
        copy_n(j, lax.rem(d + ND - j, ND)).wait_recv()
        return 0

    lax.fori_loop(1, ND, done_n, 0)
    fastest = jnp.max(jnp.max(mxd[...], axis=0), axis=(0, 1), keepdims=True)
    dt = COURANT / (fastest + 1e-6)

    def first(i, _):
        em2[i] = em[i] - dt * tend[0, i - 1]
        es2[i] = es[i] - dt * tend[1, i - 1]
        return 0

    lax.fori_loop(1, ZE - 1, first, 0)

    def step(a, c, lo):
        def body(i, _):
            t_m, t_s = tendencies(a[0], a[1], i)
            c[0][i] = a[0][i] - dt * t_m
            c[1][i] = a[1][i] - dt * t_s
            return 0

        lax.fori_loop(lo, ZE - lo, body, 0)

    step((em2, es2), (em, es), 2)
    step((em, es), (em2, es2), 3)

    def last(i, _):
        t_m, t_s = tendencies(em2, es2, i)
        out_m[i - HALO] = (em2[i] - dt * t_m)[8:40]
        out_s[i - HALO] = (es2[i] - dt * t_s)[8:40]
        return 0

    lax.fori_loop(HALO, HALO + ZL, last, 0)

    for f in drains.values():
        f()


def local(source_field, methane, sulfate, layer_of_cell, perm_horizontal, perm_vertical, vent_mask):
    hi, lo, eig_x, eig_y = tables()
    vmem = pl.BlockSpec(memory_space=pltpu.VMEM)
    smem = pl.BlockSpec(memory_space=pltpu.SMEM)
    hbm = pl.BlockSpec(memory_space=pl.ANY)
    field = jax.ShapeDtypeStruct((ZL, XL, N), F32)
    dma = pltpu.SemaphoreType.DMA
    ext = pltpu.VMEM((ZE, XE, N), F32)
    scratch = [
        pltpu.VMEM((NQ, 16, ZL * XL), F32),
        pltpu.VMEM((NQ, 16, ZL * XL), F32),
        pltpu.VMEM((ZB * 16, N), BF16),
        pltpu.VMEM((ZB * 16, N), BF16),
        pltpu.VMEM((ZB, 16, N), F32),
        pltpu.VMEM((NQ, 16, ZL * XL), F32),
        pltpu.VMEM((NQ, 16, ZL * XL), F32),
        pltpu.VMEM((16, 128), F32),
        pltpu.VMEM((NZ, 16, N), F32),
        pltpu.VMEM((NZ, 16, N), F32),
        pltpu.VMEM((NX_CHIPS, 16, N), F32),
        pltpu.VMEM((NX_CHIPS, 16, N), F32),
        pltpu.VMEM((ZB, 16, N), F32),
        pltpu.VMEM((ZB, 16, N), F32),
        pltpu.VMEM((2, 16, N), F32),
        pltpu.VMEM((NX_CHIPS, 16, N), F32),
        ext, ext, ext, ext, ext,
        pltpu.VMEM((XE, N), F32),
        pltpu.VMEM((3, 2, ZL // 2, 8, N), F32),
        pltpu.VMEM((3, 2, ZE // 2, 8, N), F32),
        pltpu.VMEM((7, ZE - 2, XE, N), F32),
        pltpu.VMEM((2, ZE - 2, XE, N), F32),
        pltpu.VMEM((2, 8, 128), F32),
        pltpu.VMEM((NH, 8, 128), F32),
        pltpu.VMEM((ND, 8, 128), F32),
        pltpu.SMEM((NZ + 1,), F32),
        pltpu.SMEM((NZ,), F32),
        dma((NQ,)), dma((NQ,)), dma((NX_CHIPS,)), dma((NX_CHIPS,)), dma((NQ,)), dma((NQ,)),
        dma((3, 8)), dma((3, 8)), dma((2,)), dma((2,)),
        dma((NH,)), dma((NH,)), dma((ND,)), dma((ND,)), dma((3,)),
    ]
    return pl.pallas_call(
        kernel,
        out_shape=(field, field, field),
        in_specs=[vmem, hbm, hbm, smem, smem, smem, vmem, vmem, vmem, vmem, hbm],
        out_specs=(vmem, vmem, vmem),
        scratch_shapes=scratch,
        compiler_params=pltpu.CompilerParams(
            collective_id=0, has_side_effects=True, vmem_limit_bytes=60 * 1024 * 1024),
    )(source_field, methane, sulfate, layer_of_cell, perm_horizontal, perm_vertical, vent_mask,
      jnp.asarray(hi), jnp.asarray(lo), jnp.asarray(eig_x), jnp.asarray(eig_y))


def solution(mesh):
    field = P("depth", "horiz", None)
    return jax.shard_map(
        local,
        mesh=mesh,
        in_specs=(field, field, field, P(), P(), P(), P("horiz", None)),
        out_specs=(field, field, field),
        check_vma=False,
    )
```

```python
import jax
import jax.numpy as jnp
import ml_dtypes
import numpy as np
from jax import lax
from jax.experimental import pallas as pl
from jax.experimental.pallas import tpu as pltpu
from jax.sharding import PartitionSpec as P

STEPS = 4
STORAGE = 0.004
COURANT = 0.5
REACTION = 4.0
VENT_INPUT = 4.0

NZ = 64
N = 512
NH = 16
ND = 8
ZL = 8
XL = 32
HALO = 4
ZE = ZL + 2 * HALO
XE = XL + 16
NX_CHIPS = 4
ZB = NZ // NX_CHIPS
NQ = 2 * NH

PLANE = sorted(
    [(z, y, c) for z in range(4) for y in range(4) for c in range(2)][1:],
    key=lambda o: -(min(o[0], 4 - o[0]) + min(o[1], 4 - o[1])))

GRID = 2

F32 = jnp.float32
BF16 = jnp.bfloat16


def tables():
    k = np.arange(N)
    angle = (k[:, None] * k[None, :] % N) * (2.0 * np.pi / N)
    cas = np.cos(angle) + np.sin(angle)
    hi = cas.astype(np.float32).astype(ml_dtypes.bfloat16)
    lo = (cas - hi.astype(np.float64)).astype(np.float32).astype(ml_dtypes.bfloat16)
    eig = (4.0 * np.sin(np.pi * k / N) ** 2).astype(np.float32)
    eig_x = np.broadcast_to(eig.reshape(1, N), (16, N)).copy()
    eig_y = np.broadcast_to(eig.reshape(NQ, 16, 1), (NQ, 16, 128)).copy()
    return hi, lo, eig_x, eig_y


def split(v):
    hi = v.astype(BF16)
    return hi, (v - hi.astype(F32)).astype(BF16)


def dot3(a, b, dims=((1,), (0,))):
    (ah, al), (bh, bl) = a, b
    d = lambda x, y: lax.dot_general(x, y, (dims, ((), ())), preferred_element_type=F32)
    return d(ah, bh) + (d(al, bh) + d(ah, bl))


def kernel(
    src_in, met, sul, layer, ph, pv, vent_in, hhi_in, hlo_in, eig_x_in, eig_y,
    out_p, out_m, out_s,
    src, vent, hhi, hlo, eig_x, res_m, res_s,
    y1, r1, ah, al, fz, w1, y4, ey,
    inv_d, inv_u, prod_d, prod_u, gd, pi, send_a, recv_a,
    ep, em, es, em2, es2, ev, pack, xin, coef, tend,
    mx, mxh, mxd, cpl, khs,
    s1, q1, s2, q2, s4, q4, hs, hq, vs, vq, ms, mq, ns, nq, lsem,
):
    h = lax.axis_index("horiz")
    d = lax.axis_index("depth")
    chip = lax.div(d, 2)
    core = lax.rem(d, 2)
    q = h * 2 + core

    drains = {}

    def dev(hh, dd):
        return {"horiz": hh, "depth": dd}

    def mate(j):
        return lax.rem(h + j, NH)

    hz, hy = lax.div(h, 4), lax.rem(h, 4)

    def fellow(j, sign=1):
        dz, dy, dc = PLANE[j]
        fh = lax.rem(hz + sign * dz + 4, 4) * 4 + lax.rem(hy + sign * dy + 4, 4)
        fc = lax.rem(core + dc, 2)
        return 2 * fh + fc, fh, fc

    def slot(oq):
        return lax.rem(oq, 2) * NH + lax.div(oq, 2)

    h_up, h_dn = lax.rem(h + 1, NH), lax.rem(h + NH - 1, NH)
    d_up, d_dn = lax.rem(d + 1, ND), lax.rem(d + ND - 1, ND)

    first_loads = [
        pltpu.make_async_copy(src_in, src, lsem.at[3]),
        pltpu.make_async_copy(hhi_in, hhi, lsem.at[4]),
        pltpu.make_async_copy(hlo_in, hlo, lsem.at[5]),
    ]
    for c in first_loads:
        c.start()

    barrier = pltpu.get_barrier_semaphore()

    for j in range(NQ - 1):
        _, fh, fc = fellow(j)
        pl.semaphore_signal(barrier, inc=1, device_id=dev(fh, 2 * chip + fc))

    def greet_d(j, _):
        pl.semaphore_signal(barrier, inc=1, device_id=dev(h, lax.rem(d + j, ND)))
        return 0

    lax.fori_loop(1, ND, greet_d, 0)
    for hh in (h_up, h_dn):
        for dd in (d_up, d_dn):
            pl.semaphore_signal(barrier, inc=1, device_id=dev(hh, dd))

    own_copies = [
        pltpu.make_async_copy(met, em.at[pl.ds(HALO, ZL), pl.ds(8, XL)], lsem.at[0]),
        pltpu.make_async_copy(sul, es.at[pl.ds(HALO, ZL), pl.ds(8, XL)], lsem.at[1]),
        pltpu.make_async_copy(eig_y.at[q], ey, lsem.at[2]),
        pltpu.make_async_copy(vent_in, vent, lsem.at[6]),
        pltpu.make_async_copy(eig_x_in, eig_x, lsem.at[7]),
    ]
    for c in own_copies:
        c.start()
    drains["own"] = lambda: [c.wait() for c in own_copies]

    for c in first_loads:
        c.wait()
    s = split(src[...].reshape(ZL * XL, N))
    for n in range(2):
        rows = (hhi[256 * n:256 * n + 256], hlo[256 * n:256 * n + 256])
        y1[16 * n:16 * n + 16] = dot3(rows, s, ((1,), (1,))).reshape(16, 16, ZL * XL)

    pl.semaphore_wait(barrier, (NQ - 1) + (ND - 1) + 4)

    def copy1(j, oq):
        pq, fh, fc = fellow(j)
        return pltpu.make_async_remote_copy(
            src_ref=y1.at[pq], dst_ref=r1.at[slot(oq)],
            send_sem=s1.at[j], recv_sem=q1.at[j], device_id=dev(fh, 2 * chip + fc))

    def go1():
        for j in range(NQ - 1):
            copy1(j, q).start()

    go1()
    def left1():
        for j in range(NQ - 1):
            copy1(j, q).wait_send()
    drains["1"] = left1

    def halo_copies(f, ref, dirs):
        own = pl.ds(8, XL)
        lo_p, hi_p = pack.at[f, 0], pack.at[f, 1]
        plan = (
            (ref.at[pl.ds(8, 4), own], ref.at[pl.ds(0, 4), own], h, d_up),
            (ref.at[pl.ds(4, 4), own], ref.at[pl.ds(12, 4), own], h, d_dn),
            (hi_p, xin.at[f, 0, pl.ds(2, 4)], h_up, d),
            (lo_p, xin.at[f, 1, pl.ds(2, 4)], h_dn, d),
            (hi_p.at[pl.ds(2, 2)], xin.at[f, 0, pl.ds(0, 2)], h_up, d_up),
            (hi_p.at[pl.ds(0, 2)], xin.at[f, 0, pl.ds(6, 2)], h_up, d_dn),
            (lo_p.at[pl.ds(2, 2)], xin.at[f, 1, pl.ds(0, 2)], h_dn, d_up),
            (lo_p.at[pl.ds(0, 2)], xin.at[f, 1, pl.ds(6, 2)], h_dn, d_dn),
            (ref.at[pl.ds(11, 1), own], ref.at[pl.ds(3, 1), own], h, d_up),
            (ref.at[pl.ds(4, 1), own], ref.at[pl.ds(12, 1), own], h, d_dn),
            (ref.at[pl.ds(8, 3), own], ref.at[pl.ds(0, 3), own], h, d_up),
            (ref.at[pl.ds(5, 3), own], ref.at[pl.ds(13, 3), own], h, d_dn),
        )
        return [
            pltpu.make_async_remote_copy(
                src_ref=plan[i][0], dst_ref=plan[i][1], send_sem=hs.at[f, i], recv_sem=hq.at[f, i],
                device_id=dev(plan[i][2], plan[i][3]))
            for i in dirs
        ]

    sub8 = lax.broadcasted_iota(jnp.int32, (8, N), 0)

    def pack_rows(f, ref):
        for zz in range(ZL // 2):
            even, odd = ref[HALO + 2 * zz], ref[HALO + 2 * zz + 1]
            pack[f, 0, zz] = jnp.where(sub8 < 4, even[8:16], pltpu.roll(odd[8:16], 4, 0))
            pack[f, 1, zz] = jnp.where(sub8 >= 4, even[32:40], pltpu.roll(odd[32:40], 4, 0))

    def unpack_rows(f, ref, pairs=range(ZE // 2)):
        for zz in pairs:
            for side, row in ((0, 0), (1, 40)):
                tile = xin[f, side, zz]
                ref[2 * zz, row:row + 8] = tile
                ref[2 * zz + 1, row:row + 8] = pltpu.roll(tile, 4, 0)

    def table(z, _):
        khs[z] = ph[layer[z]]
        return 0

    lax.fori_loop(0, NZ, table, 0)
    cpl[0] = 0.0
    cpl[NZ] = 0.0

    def face(i, _):
        a, c = pv[layer[i - 1]], pv[layer[i]]
        cpl[i] = 2.0 * a * c / (a + c)
        return 0

    lax.fori_loop(1, NZ, face, 0)

    drains.pop("own")()
    conc = ((1, em), (2, es))
    for f, ref in conc:
        for c in halo_copies(f, ref, (0, 1)):
            c.start()
    drains["c01"] = lambda: [c.wait() for f, ref in conc for c in halo_copies(f, ref, (0, 1))]
    for f, ref in conc:
        pack_rows(f, ref)
    ev[8:40] = vent[...].astype(F32)
    vent_copies = [
        pltpu.make_async_remote_copy(
            src_ref=ev.at[pl.ds(32, 8)], dst_ref=ev.at[pl.ds(0, 8)],
            send_sem=vs.at[0], recv_sem=vq.at[0], device_id=dev(h_up, d)),
        pltpu.make_async_remote_copy(
            src_ref=ev.at[pl.ds(8, 8)], dst_ref=ev.at[pl.ds(40, 8)],
            send_sem=vs.at[1], recv_sem=vq.at[1], device_id=dev(h_dn, d)),
    ]

    lam = eig_x[...] + jnp.concatenate([ey[...]] * 4, axis=1)
    blank = jnp.zeros((16, N), F32)
    state = (blank, blank)
    for j in range(NX_CHIPS):
        def factor(i, carry, j=j):
            rd, ru, bd, bu = carry
            z, y = ZB * j + i, NZ - 1 - ZB * j - i
            cu, cd = cpl[z], cpl[z + 1]
            v = 1.0 / ((cu + cd + khs[z] * lam + STORAGE) - cu * rd)
            inv_d[z] = v
            rd, bd = cd * v, bd * (cu * v)
            cu, cd = cpl[y], cpl[y + 1]
            v = 1.0 / ((cu + cd + khs[y] * lam + STORAGE) - cd * ru)
            inv_u[y] = v
            ru, bu = cu * v, bu * (cd * v)
            return rd, ru, bd, bu

        rd, ru, bd, bu = lax.fori_loop(0, ZB, factor, state + (blank + 1.0, blank + 1.0))
        state = (rd, ru)
        prod_d[j] = bd
        prod_u[NX_CHIPS - 1 - j] = bu
    base = ZB * chip

    def product(i, v):
        v = v * (cpl[base + i] * inv_d[base + i])
        pi[i] = v
        return v

    lax.fori_loop(0, ZB, product, blank + 1.0)
    r_last = cpl[base + ZB] * inv_d[base + ZB - 1]
    r_next = cpl[base + ZB] * inv_u[jnp.minimum(base + ZB, NZ - 1)]
    join = 1.0 / (1.0 - r_last * r_next)

    r1[slot(q)] = y1[q]

    for j in range(NQ - 1):
        copy1(j, fellow(j, -1)[0]).wait_recv()
    for f, ref in conc:
        for c in halo_copies(f, ref, range(2, 8)):
            c.start()
    for c in vent_copies:
        c.start()
    drains["c28"] = lambda: [c.wait() for c in vent_copies + [c for f, ref in conc for c in halo_copies(f, ref, range(2, 8))]]

    group = lax.broadcasted_iota(jnp.int32, (16, 128), 1) // 32

    def regroup(v):
        lower, even = group < 2, lax.rem(group, 2) == 0
        p = [jnp.where(lower, v[i], pltpu.roll(v[i + 2], 64, 1)) for i in range(2)]
        r = [jnp.where(lower, pltpu.roll(v[i], 64, 1), v[i + 2]) for i in range(2)]
        out = []
        for a, b in (p, r):
            out.append(jnp.where(even, a, pltpu.roll(b, 32, 1)))
            out.append(jnp.where(even, pltpu.roll(a, 96, 1), b))
        return out

    for c in range(2):
        for g in range(2):
            for t in range(4):
                v = regroup([r1[NH * c + 4 * t + i, :, 128 * g:128 * g + 128] for i in range(4)])
                for i in range(4):
                    row = 16 * (8 * c + 4 * g + i)
                    hi, lo = split(v[i])
                    ah[row:row + 16, 128 * t:128 * t + 128] = hi
                    al[row:row + 16, 128 * t:128 * t + 128] = lo
    for n in range(2):
        cols = (hhi[:, 256 * n:256 * n + 256], hlo[:, 256 * n:256 * n + 256])
        o = dot3((ah[...], al[...]), cols)
        fz[:, :, 256 * n:256 * n + 256] = (o * (1.0 / (N * N))).reshape(ZB, 16, 256)

    def down(i, v):
        k = inv_d[base + i]
        v = fz[i] * k + (cpl[base + i] * k) * v
        gd[i] = v
        return v

    def upward(n, v):
        i = ZB - 1 - n
        k = inv_u[base + i]
        return fz[i] * k + (cpl[base + i + 1] * k) * v

    send_a[0] = lax.fori_loop(0, ZB, down, blank, unroll=4)
    send_a[1] = lax.fori_loop(0, ZB, upward, blank, unroll=4)

    def copy2(j, origin):
        to = lax.rem(chip + j, NX_CHIPS)
        return pltpu.make_async_remote_copy(
            src_ref=send_a.at[jnp.where(to > chip, 0, 1)], dst_ref=recv_a.at[origin],
            send_sem=s2.at[j], recv_sem=q2.at[j], device_id=dev(h, 2 * to + core))

    def go2(j, _):
        copy2(j, chip).start()
        return 0

    lax.fori_loop(1, NX_CHIPS, go2, 0)

    def left2(j, _):
        copy2(j, chip).wait_send()
        return 0

    drains["2"] = lambda: lax.fori_loop(1, NX_CHIPS, left2, 0)
    recv_a[chip] = blank

    def done2(j, _):
        copy2(j, lax.rem(chip + NX_CHIPS - j, NX_CHIPS)).wait_recv()
        return 0

    lax.fori_loop(1, NX_CHIPS, done2, 0)
    from_top, from_bottom = blank, blank
    for j in range(NX_CHIPS - 1):
        from_top = jnp.where(j < chip, recv_a[j] + prod_d[j] * from_top, from_top)
        k = NX_CHIPS - 1 - j
        from_bottom = jnp.where(k > chip, recv_a[k] + prod_u[k] * from_bottom, from_bottom)

    def solved(i, p):
        row = pl.ds(pl.multiple_of(16 * i, 16), 16)
        hi, lo = split(p)
        ah[row, :] = hi
        al[row, :] = lo

    p = (gd[ZB - 1] + pi[ZB - 1] * from_top + r_last * from_bottom) * join
    solved(ZB - 1, p)

    def up(n, p):
        i = ZB - 2 - n
        p = gd[i] + pi[i] * from_top + (cpl[base + i + 1] * inv_d[base + i]) * p
        solved(i, p)
        return p

    lax.fori_loop(0, ZB - 1, up, p)
    for n in range(2):
        cols = (hhi[:, 256 * n:256 * n + 256], hlo[:, 256 * n:256 * n + 256])
        fz[:, :, 256 * n:256 * n + 256] = dot3((ah[...], al[...]), cols).reshape(ZB, 16, 256)
    for c in range(2):
        for g in range(2):
            for t in range(4):
                v = regroup([fz[8 * c + 4 * g + i, :, 128 * t:128 * t + 128] for i in range(4)])
                for i in range(4):
                    w1[NH * c + 4 * t + i, :, 128 * g:128 * g + 128] = v[i]

    def copy4(j, oq):
        pq, fh, fc = fellow(j)
        return pltpu.make_async_remote_copy(
            src_ref=w1.at[slot(pq)], dst_ref=y4.at[oq],
            send_sem=s4.at[j], recv_sem=q4.at[j], device_id=dev(fh, 2 * chip + fc))

    def go4():
        for j in range(NQ - 1):
            copy4(j, q).start()

    go4()

    def left4():
        for j in range(NQ - 1):
            copy4(j, q).wait_send()

    drains["4"] = left4
    y4[q] = w1[slot(q)]

    del drains["c01"], drains["c28"]
    for f, ref in conc:
        for c in halo_copies(f, ref, range(8)):
            c.wait()
        unpack_rows(f, ref)
    for c in vent_copies:
        c.wait()

    for j in range(NQ - 1):
        copy4(j, fellow(j, -1)[0]).wait_recv()

    s = split(y4[...].reshape(N, ZL * XL).T)
    for n in range(2):
        o = dot3(s, (hhi[:, 256 * n:256 * n + 256], hlo[:, 256 * n:256 * n + 256]))
        ep[HALO:HALO + ZL, 8:40, 256 * n:256 * n + 256] = o.reshape(ZL, XL, 256)
    outs = [pltpu.make_async_copy(ep.at[pl.ds(HALO, ZL), pl.ds(8, XL)], out_p, lsem.at[8])]
    outs[0].start()
    drains["out"] = lambda: [c.wait() for c in outs]

    near = halo_copies(0, ep, (8, 9, 2, 3))
    rest = halo_copies(0, ep, (10, 11, 4, 5, 6, 7))
    for c in near[:2]:
        c.start()
    pack_rows(0, ep)
    for c in near[2:] + rest:
        c.start()
    drains["p"] = lambda: [c.wait_send() for c in near + rest]
    for c in near:
        c.wait_recv()
    unpack_rows(0, ep, (2, 3, 4, 5))

    def cell(i):
        gz = lax.rem(d * ZL + i + (NZ - HALO), NZ)
        kh, cu, cd = khs[gz], cpl[gz], cpl[gz + 1]
        p = ep[i]
        east = -kh * (pltpu.roll(p, XE - 1, 0) - p)
        north = -kh * (pltpu.roll(p, N - 1, 1) - p)
        above = -cu * (p - ep[i - 1])
        below = -cd * (ep[i + 1] - p)
        return east, pltpu.roll(east, 1, 0), north, pltpu.roll(north, 1, 1), above, below

    def speed(i, m):
        e, w, n, s_, a, c = [jnp.abs(v[8:40]) for v in cell(i)]
        v = e + w + n + s_ + a + c
        v = jnp.max(v.reshape(4, 8, N), axis=0)
        return jnp.maximum(m, jnp.maximum(jnp.maximum(v[:, :128], v[:, 128:256]),
                                          jnp.maximum(v[:, 256:384], v[:, 384:])))

    mx[0] = lax.fori_loop(HALO, HALO + ZL, speed, jnp.zeros((8, 128), F32))

    def copy_m(j, origin):
        return pltpu.make_async_remote_copy(
            src_ref=mx.at[0], dst_ref=mxh.at[origin], send_sem=ms.at[j], recv_sem=mq.at[j],
            device_id=dev(mate(j), d))

    def copy_n(j, origin):
        return pltpu.make_async_remote_copy(
            src_ref=mx.at[1], dst_ref=mxd.at[origin], send_sem=ns.at[j], recv_sem=nq.at[j],
            device_id=dev(h, lax.rem(d + j, ND)))

    def go_m(j, _):
        copy_m(j, h).start()
        return 0

    lax.fori_loop(1, NH, go_m, 0)
    def left_m(j, _):
        copy_m(j, h).wait_send()
        return 0
    drains["m"] = lambda: lax.fori_loop(1, NH, left_m, 0)
    mxh[h] = mx[0]

    def stencil(get, c_ref, i):
        c = c_ref[i]
        return (get(0) * c
                + get(1) * pltpu.roll(c, XE - 1, 0) + get(2) * pltpu.roll(c, 1, 0)
                + get(3) * pltpu.roll(c, N - 1, 1) + get(4) * pltpu.roll(c, 1, 1)
                + get(5) * c_ref[i + 1] + get(6) * c_ref[i - 1])

    def tendencies(m_ref, s_ref, i):
        get = lambda k: coef[k, i - 1]
        react = REACTION * m_ref[i] * s_ref[i]
        return (stencil(get, m_ref, i) + (react - VENT_INPUT * ev[...]),
                stencil(get, s_ref, i) + react)

    def prepare(i, _):
        e, w, n, s_, a, c = cell(i)
        pos, neg = (lambda v: jnp.maximum(v, 0.0)), (lambda v: jnp.minimum(v, 0.0))
        coef[0, i - 1] = (pos(e) - neg(w)) + (pos(n) - neg(s_)) + (pos(c) - neg(a))
        coef[1, i - 1] = neg(e)
        coef[2, i - 1] = -pos(w)
        coef[3, i - 1] = neg(n)
        coef[4, i - 1] = -pos(s_)
        coef[5, i - 1] = neg(c)
        coef[6, i - 1] = -pos(a)
        t_m, t_s = tendencies(em, es, i)
        tend[0, i - 1] = t_m
        tend[1, i - 1] = t_s
        return 0

    lax.fori_loop(HALO + 1, HALO + ZL - 1, prepare, 0)
    for c in rest:
        c.wait_recv()
    unpack_rows(0, ep, (0, 1, 6, 7))
    lax.fori_loop(2, HALO + 1, prepare, 0)

    def done_m(j, _):
        copy_m(j, lax.rem(h + NH - j, NH)).wait_recv()
        return 0

    lax.fori_loop(1, NH, done_m, 0)
    mx[1] = jnp.max(mxh[...], axis=0)

    def go_n(j, _):
        copy_n(j, d).start()
        return 0

    lax.fori_loop(1, ND, go_n, 0)
    def left_n(j, _):
        copy_n(j, d).wait_send()
        return 0
    drains["n"] = lambda: lax.fori_loop(1, ND, left_n, 0)
    mxd[d] = mx[1]

    prepare(1, 0)
    lax.fori_loop(HALO + ZL - 1, ZE - 1, prepare, 0)

    def done_n(j, _):
        copy_n(j, lax.rem(d + ND - j, ND)).wait_recv()
        return 0

    lax.fori_loop(1, ND, done_n, 0)
    fastest = jnp.max(jnp.max(mxd[...], axis=0), axis=(0, 1), keepdims=True)
    dt = COURANT / (fastest + 1e-6)

    def first(i, _):
        em2[i] = em[i] - dt * tend[0, i - 1]
        es2[i] = es[i] - dt * tend[1, i - 1]
        return 0

    lax.fori_loop(1, ZE - 1, first, 0)

    def step(a, c, lo):
        def body(i, _):
            t_m, t_s = tendencies(a[0], a[1], i)
            c[0][i] = a[0][i] - dt * t_m
            c[1][i] = a[1][i] - dt * t_s
            return 0

        lax.fori_loop(lo, ZE - lo, body, 0)

    step((em2, es2), (em, es), 2)
    step((em, es), (em2, es2), 3)

    def last(i, _):
        t_m, t_s = tendencies(em2, es2, i)
        res_m[i - HALO] = (em2[i] - dt * t_m)[8:40]
        res_s[i - HALO] = (es2[i] - dt * t_s)[8:40]
        return 0

    lax.fori_loop(HALO, HALO + ZL, last, 0)
    for k, (ref, out) in enumerate(((res_m, out_m), (res_s, out_s))):
        outs.append(pltpu.make_async_copy(ref, out, lsem.at[9 + k]))
        outs[-1].start()

    for f in drains.values():
        f()


def deliver(p, m, s, out_p, out_m, out_s):
    out_p[...] = p[...]
    out_m[...] = m[...]
    out_s[...] = s[...]


def local(source_field, methane, sulfate, layer_of_cell, perm_horizontal, perm_vertical, vent_mask):
    hi, lo, eig_x, eig_y = tables()
    smem = pl.BlockSpec(memory_space=pltpu.SMEM)
    hbm = pl.BlockSpec(memory_space=pl.ANY)
    field = jax.ShapeDtypeStruct((ZL, XL, N), F32)
    dma = pltpu.SemaphoreType.DMA
    ext = pltpu.VMEM((ZE, XE, N), F32)
    scratch = [
        pltpu.VMEM((ZL, XL, N), F32),
        pltpu.VMEM((XL, N), jnp.int32),
        pltpu.VMEM((N, N), BF16),
        pltpu.VMEM((N, N), BF16),
        pltpu.VMEM((16, N), F32),
        pltpu.VMEM((ZL, XL, N), F32),
        pltpu.VMEM((ZL, XL, N), F32),
        pltpu.VMEM((NQ, 16, ZL * XL), F32),
        pltpu.VMEM((NQ, 16, ZL * XL), F32),
        pltpu.VMEM((ZB * 16, N), BF16),
        pltpu.VMEM((ZB * 16, N), BF16),
        pltpu.VMEM((ZB, 16, N), F32),
        pltpu.VMEM((NQ, 16, ZL * XL), F32),
        pltpu.VMEM((NQ, 16, ZL * XL), F32),
        pltpu.VMEM((16, 128), F32),
        pltpu.VMEM((NZ, 16, N), F32),
        pltpu.VMEM((NZ, 16, N), F32),
        pltpu.VMEM((NX_CHIPS, 16, N), F32),
        pltpu.VMEM((NX_CHIPS, 16, N), F32),
        pltpu.VMEM((ZB, 16, N), F32),
        pltpu.VMEM((ZB, 16, N), F32),
        pltpu.VMEM((2, 16, N), F32),
        pltpu.VMEM((NX_CHIPS, 16, N), F32),
        ext, ext, ext, ext, ext,
        pltpu.VMEM((XE, N), F32),
        pltpu.VMEM((3, 2, ZL // 2, 8, N), F32),
        pltpu.VMEM((3, 2, ZE // 2, 8, N), F32),
        pltpu.VMEM((7, ZE - 2, XE, N), F32),
        pltpu.VMEM((2, ZE - 2, XE, N), F32),
        pltpu.VMEM((2, 8, 128), F32),
        pltpu.VMEM((NH, 8, 128), F32),
        pltpu.VMEM((ND, 8, 128), F32),
        pltpu.SMEM((NZ + 1,), F32),
        pltpu.SMEM((NZ,), F32),
        dma((NQ,)), dma((NQ,)), dma((NX_CHIPS,)), dma((NX_CHIPS,)), dma((NQ,)), dma((NQ,)),
        dma((3, 12)), dma((3, 12)), dma((2,)), dma((2,)),
        dma((NH,)), dma((NH,)), dma((ND,)), dma((ND,)), dma((11,)),
    ]
    results = pl.pallas_call(
        kernel,
        out_shape=(field, field, field),
        in_specs=[hbm, hbm, hbm, smem, smem, smem, hbm, hbm, hbm, hbm, hbm],
        out_specs=(hbm, hbm, hbm),
        scratch_shapes=scratch,
        compiler_params=pltpu.CompilerParams(
            collective_id=0, has_side_effects=True, vmem_limit_bytes=60 * 1024 * 1024),
    )(source_field, methane, sulfate, layer_of_cell, perm_horizontal, perm_vertical, vent_mask,
      jnp.asarray(hi), jnp.asarray(lo), jnp.asarray(eig_x), jnp.asarray(eig_y))
    block = pl.BlockSpec((ZL // GRID, XL, N), lambda i: (i, 0, 0))
    return pl.pallas_call(
        deliver,
        grid=(GRID,),
        out_shape=(field, field, field),
        in_specs=[block] * 3,
        out_specs=(block,) * 3,
    )(*results)


def solution(mesh):
    field = P("depth", "horiz", None)
    return jax.shard_map(
        local,
        mesh=mesh,
        in_specs=(field, field, field, P(), P(), P(), P("horiz", None)),
        out_specs=(field, field, field),
        check_vma=False,
    )
```

```python
import jax
import jax.numpy as jnp
import ml_dtypes
import numpy as np
from jax import lax
from jax.experimental import pallas as pl
from jax.experimental.pallas import tpu as pltpu
from jax.sharding import PartitionSpec as P

STEPS = 4
STORAGE = 0.004
COURANT = 0.5
REACTION = 4.0
VENT_INPUT = 4.0

NZ = 64
N = 512
NH = 16
ND = 8
ZL = 8
XL = 32
HALO = 4
ZE = ZL + 2 * HALO
XE = XL + 2 * HALO
NX_CHIPS = 4
ZB = NZ // NX_CHIPS
NQ = 2 * NH

PLANE = sorted(
    [(z, y, c) for z in range(4) for y in range(4) for c in range(2)][1:],
    key=lambda o: -(min(o[0], 4 - o[0]) + min(o[1], 4 - o[1])))

PARTS = 2

F32 = jnp.float32
BF16 = jnp.bfloat16


def tables():
    k = np.arange(N)
    angle = (k[:, None] * k[None, :] % N) * (2.0 * np.pi / N)
    cas = np.cos(angle) + np.sin(angle)
    hi = cas.astype(np.float32).astype(ml_dtypes.bfloat16)
    lo = (cas - hi.astype(np.float64)).astype(np.float32).astype(ml_dtypes.bfloat16)
    eig = (4.0 * np.sin(np.pi * k / N) ** 2).astype(np.float32)
    eig_x = np.broadcast_to(eig.reshape(1, N), (16, N)).copy()
    eig_y = np.broadcast_to(eig.reshape(NQ, 16, 1), (NQ, 16, 128)).copy()
    return hi, lo, eig_x, eig_y


def split(v):
    hi = v.astype(BF16)
    return hi, (v - hi.astype(F32)).astype(BF16)


def dot3(a, b, dims=((1,), (0,))):
    (ah, al), (bh, bl) = a, b
    d = lambda x, y: lax.dot_general(x, y, (dims, ((), ())), preferred_element_type=F32)
    return d(ah, bh) + (d(al, bh) + d(ah, bl))


def kernel(
    src_in, met, sul, layer, ph, pv, vent_in, hhi_in, hlo_in, eig_x_in, eig_y,
    out_p, out_m, out_s,
    src, vent, hhi, hlo, eig_x, res_m, res_s,
    y1, r1, ah, al, fz, w1, y4, ey,
    inv_d, inv_u, prod_d, prod_u, gd, pi, send_a, recv_a,
    ep, em, es, em2, es2, ev, vin, pack, xin, coef, tend, curve,
    mx, mxh, mxd, cpl, khs,
    s1, q1, s2, q2, s4, q4, hs, hq, vs, vq, ms, mq, ns, nq, lsem,
):
    h = lax.axis_index("horiz")
    d = lax.axis_index("depth")
    chip = lax.div(d, 2)
    core = lax.rem(d, 2)
    q = h * 2 + core

    drains = {}

    def dev(hh, dd):
        return {"horiz": hh, "depth": dd}

    def mate(j):
        return lax.rem(h + j, NH)

    hz, hy = lax.div(h, 4), lax.rem(h, 4)

    def fellow(j, sign=1):
        dz, dy, dc = PLANE[j]
        fh = lax.rem(hz + sign * dz + 4, 4) * 4 + lax.rem(hy + sign * dy + 4, 4)
        fc = lax.rem(core + dc, 2)
        return 2 * fh + fc, fh, fc

    def slot(oq):
        return lax.rem(oq, 2) * NH + lax.div(oq, 2)

    h_up, h_dn = lax.rem(h + 1, NH), lax.rem(h + NH - 1, NH)
    d_up, d_dn = lax.rem(d + 1, ND), lax.rem(d + ND - 1, ND)

    first_loads = [
        pltpu.make_async_copy(src_in, src, lsem.at[3]),
        pltpu.make_async_copy(hhi_in, hhi, lsem.at[4]),
        pltpu.make_async_copy(hlo_in, hlo, lsem.at[5]),
    ]
    for c in first_loads:
        c.start()

    barrier = pltpu.get_barrier_semaphore()

    for j in range(NQ - 1):
        _, fh, fc = fellow(j)
        pl.semaphore_signal(barrier, inc=1, device_id=dev(fh, 2 * chip + fc))

    def greet_d(j, _):
        pl.semaphore_signal(barrier, inc=1, device_id=dev(h, lax.rem(d + j, ND)))
        return 0

    lax.fori_loop(1, ND, greet_d, 0)
    for hh in (h_up, h_dn):
        for dd in (d_up, d_dn):
            pl.semaphore_signal(barrier, inc=1, device_id=dev(hh, dd))

    own_copies = [
        pltpu.make_async_copy(met, em.at[pl.ds(HALO, ZL), pl.ds(0, XL)], lsem.at[0]),
        pltpu.make_async_copy(sul, es.at[pl.ds(HALO, ZL), pl.ds(0, XL)], lsem.at[1]),
        pltpu.make_async_copy(eig_y.at[q], ey, lsem.at[2]),
        pltpu.make_async_copy(vent_in, vent, lsem.at[6]),
        pltpu.make_async_copy(eig_x_in, eig_x, lsem.at[7]),
    ]
    for c in own_copies:
        c.start()
    drains["own"] = lambda: [c.wait() for c in own_copies]

    for c in first_loads:
        c.wait()
    s = split(src[...].reshape(ZL * XL, N))
    for n in range(2):
        rows = (hhi[256 * n:256 * n + 256], hlo[256 * n:256 * n + 256])
        y1[16 * n:16 * n + 16] = dot3(rows, s, ((1,), (1,))).reshape(16, 16, ZL * XL)

    pl.semaphore_wait(barrier, (NQ - 1) + (ND - 1) + 4)

    def copy1(j, oq):
        pq, fh, fc = fellow(j)
        return pltpu.make_async_remote_copy(
            src_ref=y1.at[pq], dst_ref=r1.at[slot(oq)],
            send_sem=s1.at[j], recv_sem=q1.at[j], device_id=dev(fh, 2 * chip + fc))

    def go1():
        for j in range(NQ - 1):
            copy1(j, q).start()

    go1()
    def left1():
        for j in range(NQ - 1):
            copy1(j, q).wait_send()
    drains["1"] = left1

    def halo_copies(f, ref, dirs):
        own = pl.ds(0, XL)
        lo_p, hi_p = pack.at[f, 0], pack.at[f, 1]
        plan = (
            (ref.at[pl.ds(8, 4), own], ref.at[pl.ds(0, 4), own], h, d_up),
            (ref.at[pl.ds(4, 4), own], ref.at[pl.ds(12, 4), own], h, d_dn),
            (hi_p, xin.at[f, 0, pl.ds(2, 4)], h_up, d),
            (lo_p, xin.at[f, 1, pl.ds(2, 4)], h_dn, d),
            (hi_p.at[pl.ds(2, 2)], xin.at[f, 0, pl.ds(0, 2)], h_up, d_up),
            (hi_p.at[pl.ds(0, 2)], xin.at[f, 0, pl.ds(6, 2)], h_up, d_dn),
            (lo_p.at[pl.ds(2, 2)], xin.at[f, 1, pl.ds(0, 2)], h_dn, d_up),
            (lo_p.at[pl.ds(0, 2)], xin.at[f, 1, pl.ds(6, 2)], h_dn, d_dn),
            (ref.at[pl.ds(11, 1), own], ref.at[pl.ds(3, 1), own], h, d_up),
            (ref.at[pl.ds(4, 1), own], ref.at[pl.ds(12, 1), own], h, d_dn),
            (ref.at[pl.ds(8, 3), own], ref.at[pl.ds(0, 3), own], h, d_up),
            (ref.at[pl.ds(5, 3), own], ref.at[pl.ds(13, 3), own], h, d_dn),
        )
        return [
            pltpu.make_async_remote_copy(
                src_ref=plan[i][0], dst_ref=plan[i][1], send_sem=hs.at[f, i], recv_sem=hq.at[f, i],
                device_id=dev(plan[i][2], plan[i][3]))
            for i in dirs
        ]

    sub8 = lax.broadcasted_iota(jnp.int32, (8, N), 0)

    def pack_rows(f, ref):
        for zz in range(ZL // 2):
            even, odd = ref[HALO + 2 * zz], ref[HALO + 2 * zz + 1]
            pack[f, 0, zz] = jnp.where(sub8 < 4, even[0:8], pltpu.roll(odd[0:8], 4, 0))
            pack[f, 1, zz] = jnp.where(sub8 >= 4, even[24:32], pltpu.roll(odd[24:32], 4, 0))

    def unpack_rows(f, ref, pairs=range(ZE // 2)):
        for zz in pairs:
            lower, upper = xin[f, 0, zz], xin[f, 1, zz]
            ref[2 * zz, XL:XE] = jnp.where(sub8 < 4, upper, lower)
            ref[2 * zz + 1, XL:XE] = pltpu.roll(jnp.where(sub8 < 4, lower, upper), 4, 0)

    def table(z, _):
        khs[z] = ph[layer[z]]
        return 0

    lax.fori_loop(0, NZ, table, 0)
    cpl[0] = 0.0
    cpl[NZ] = 0.0

    def face(i, _):
        a, c = pv[layer[i - 1]], pv[layer[i]]
        cpl[i] = 2.0 * a * c / (a + c)
        return 0

    lax.fori_loop(1, NZ, face, 0)

    drains.pop("own")()
    conc = ((1, em), (2, es))
    for f, ref in conc:
        for c in halo_copies(f, ref, (0, 1)):
            c.start()
    drains["c01"] = lambda: [c.wait() for f, ref in conc for c in halo_copies(f, ref, (0, 1))]
    for f, ref in conc:
        pack_rows(f, ref)
    ev[0:32] = vent[...].astype(F32)
    vent_copies = [
        pltpu.make_async_remote_copy(
            src_ref=ev.at[pl.ds(24, 8)], dst_ref=vin.at[0],
            send_sem=vs.at[0], recv_sem=vq.at[0], device_id=dev(h_up, d)),
        pltpu.make_async_remote_copy(
            src_ref=ev.at[pl.ds(0, 8)], dst_ref=vin.at[1],
            send_sem=vs.at[1], recv_sem=vq.at[1], device_id=dev(h_dn, d)),
    ]

    lam = eig_x[...] + jnp.concatenate([ey[...]] * 4, axis=1)
    blank = jnp.zeros((16, N), F32)
    state = (blank, blank)
    for j in range(NX_CHIPS):
        def factor(i, carry, j=j):
            rd, ru, bd, bu = carry
            z, y = ZB * j + i, NZ - 1 - ZB * j - i
            cu, cd = cpl[z], cpl[z + 1]
            v = 1.0 / ((cu + cd + khs[z] * lam + STORAGE) - cu * rd)
            inv_d[z] = v
            rd, bd = cd * v, bd * (cu * v)
            cu, cd = cpl[y], cpl[y + 1]
            v = 1.0 / ((cu + cd + khs[y] * lam + STORAGE) - cd * ru)
            inv_u[y] = v
            ru, bu = cu * v, bu * (cd * v)
            return rd, ru, bd, bu

        rd, ru, bd, bu = lax.fori_loop(0, ZB, factor, state + (blank + 1.0, blank + 1.0))
        state = (rd, ru)
        prod_d[j] = bd
        prod_u[NX_CHIPS - 1 - j] = bu
    base = ZB * chip

    def product(i, v):
        v = v * (cpl[base + i] * inv_d[base + i])
        pi[i] = v
        return v

    lax.fori_loop(0, ZB, product, blank + 1.0)
    r_last = cpl[base + ZB] * inv_d[base + ZB - 1]
    r_next = cpl[base + ZB] * inv_u[jnp.minimum(base + ZB, NZ - 1)]
    join = 1.0 / (1.0 - r_last * r_next)

    r1[slot(q)] = y1[q]

    for j in range(NQ - 1):
        copy1(j, fellow(j, -1)[0]).wait_recv()
    for f, ref in conc:
        for c in halo_copies(f, ref, range(2, 8)):
            c.start()
    for c in vent_copies:
        c.start()
    drains["c28"] = lambda: [c.wait() for c in vent_copies + [c for f, ref in conc for c in halo_copies(f, ref, range(2, 8))]]

    group = lax.broadcasted_iota(jnp.int32, (16, 128), 1) // 32

    def regroup(v):
        lower, even = group < 2, lax.rem(group, 2) == 0
        p = [jnp.where(lower, v[i], pltpu.roll(v[i + 2], 64, 1)) for i in range(2)]
        r = [jnp.where(lower, pltpu.roll(v[i], 64, 1), v[i + 2]) for i in range(2)]
        out = []
        for a, b in (p, r):
            out.append(jnp.where(even, a, pltpu.roll(b, 32, 1)))
            out.append(jnp.where(even, pltpu.roll(a, 96, 1), b))
        return out

    for c in range(2):
        for g in range(2):
            for t in range(4):
                v = regroup([r1[NH * c + 4 * t + i, :, 128 * g:128 * g + 128] for i in range(4)])
                for i in range(4):
                    row = 16 * (8 * c + 4 * g + i)
                    hi, lo = split(v[i])
                    ah[row:row + 16, 128 * t:128 * t + 128] = hi
                    al[row:row + 16, 128 * t:128 * t + 128] = lo
    for n in range(2):
        cols = (hhi[:, 256 * n:256 * n + 256], hlo[:, 256 * n:256 * n + 256])
        o = dot3((ah[...], al[...]), cols)
        fz[:, :, 256 * n:256 * n + 256] = (o * (1.0 / (N * N))).reshape(ZB, 16, 256)

    def down(i, v):
        k = inv_d[base + i]
        v = fz[i] * k + (cpl[base + i] * k) * v
        gd[i] = v
        return v

    def upward(n, v):
        i = ZB - 1 - n
        k = inv_u[base + i]
        return fz[i] * k + (cpl[base + i + 1] * k) * v

    send_a[0] = lax.fori_loop(0, ZB, down, blank, unroll=4)
    send_a[1] = lax.fori_loop(0, ZB, upward, blank, unroll=4)

    def copy2(j, origin):
        to = lax.rem(chip + j, NX_CHIPS)
        return pltpu.make_async_remote_copy(
            src_ref=send_a.at[jnp.where(to > chip, 0, 1)], dst_ref=recv_a.at[origin],
            send_sem=s2.at[j], recv_sem=q2.at[j], device_id=dev(h, 2 * to + core))

    def go2(j, _):
        copy2(j, chip).start()
        return 0

    lax.fori_loop(1, NX_CHIPS, go2, 0)

    def left2(j, _):
        copy2(j, chip).wait_send()
        return 0

    drains["2"] = lambda: lax.fori_loop(1, NX_CHIPS, left2, 0)
    recv_a[chip] = blank

    def done2(j, _):
        copy2(j, lax.rem(chip + NX_CHIPS - j, NX_CHIPS)).wait_recv()
        return 0

    lax.fori_loop(1, NX_CHIPS, done2, 0)
    from_top, from_bottom = blank, blank
    for j in range(NX_CHIPS - 1):
        from_top = jnp.where(j < chip, recv_a[j] + prod_d[j] * from_top, from_top)
        k = NX_CHIPS - 1 - j
        from_bottom = jnp.where(k > chip, recv_a[k] + prod_u[k] * from_bottom, from_bottom)

    def solved(i, p):
        row = pl.ds(pl.multiple_of(16 * i, 16), 16)
        hi, lo = split(p)
        ah[row, :] = hi
        al[row, :] = lo

    p = (gd[ZB - 1] + pi[ZB - 1] * from_top + r_last * from_bottom) * join
    solved(ZB - 1, p)

    def up(n, p):
        i = ZB - 2 - n
        p = gd[i] + pi[i] * from_top + (cpl[base + i + 1] * inv_d[base + i]) * p
        solved(i, p)
        return p

    lax.fori_loop(0, ZB - 1, up, p)
    for n in range(2):
        cols = (hhi[:, 256 * n:256 * n + 256], hlo[:, 256 * n:256 * n + 256])
        fz[:, :, 256 * n:256 * n + 256] = dot3((ah[...], al[...]), cols).reshape(ZB, 16, 256)
    for c in range(2):
        for g in range(2):
            for t in range(4):
                v = regroup([fz[8 * c + 4 * g + i, :, 128 * t:128 * t + 128] for i in range(4)])
                for i in range(4):
                    w1[NH * c + 4 * t + i, :, 128 * g:128 * g + 128] = v[i]

    def copy4(j, oq):
        pq, fh, fc = fellow(j)
        return pltpu.make_async_remote_copy(
            src_ref=w1.at[slot(pq)], dst_ref=y4.at[oq],
            send_sem=s4.at[j], recv_sem=q4.at[j], device_id=dev(fh, 2 * chip + fc))

    def go4():
        for j in range(NQ - 1):
            copy4(j, q).start()

    go4()

    def left4():
        for j in range(NQ - 1):
            copy4(j, q).wait_send()

    drains["4"] = left4
    y4[q] = w1[slot(q)]

    del drains["c01"], drains["c28"]
    for f, ref in conc:
        for c in halo_copies(f, ref, range(8)):
            c.wait()
        unpack_rows(f, ref)
    for c in vent_copies:
        c.wait()
    ev[XL:XE] = jnp.where(sub8 < 4, vin[1], vin[0])

    for j in range(NQ - 1):
        copy4(j, fellow(j, -1)[0]).wait_recv()

    s = split(y4[...].reshape(N, ZL * XL).T)
    for n in range(2):
        o = dot3(s, (hhi[:, 256 * n:256 * n + 256], hlo[:, 256 * n:256 * n + 256]))
        ep[HALO:HALO + ZL, 0:32, 256 * n:256 * n + 256] = o.reshape(ZL, XL, 256)
    outs = [pltpu.make_async_copy(ep.at[pl.ds(HALO, ZL), pl.ds(0, XL)], out_p, lsem.at[8])]
    outs[0].start()
    drains["out"] = lambda: [c.wait() for c in outs]

    near = halo_copies(0, ep, (8, 9, 2, 3))
    rest = halo_copies(0, ep, (10, 11, 4, 5, 6, 7))
    for c in near[:2]:
        c.start()
    pack_rows(0, ep)
    for c in near[2:] + rest:
        c.start()
    drains["p"] = lambda: [c.wait_send() for c in near + rest]
    drains["pr"] = lambda: [c.wait_recv() for c in rest]
    for c in near:
        c.wait_recv()
    unpack_rows(0, ep, (2, 3, 4, 5))

    def cell(i):
        gz = lax.rem(d * ZL + i + (NZ - HALO), NZ)
        kh, cu, cd = khs[gz], cpl[gz], cpl[gz + 1]
        p = ep[i]
        east = -kh * (pltpu.roll(p, XE - 1, 0) - p)
        north = -kh * (pltpu.roll(p, N - 1, 1) - p)
        above = -cu * (p - ep[i - 1])
        below = -cd * (ep[i + 1] - p)
        return east, pltpu.roll(east, 1, 0), north, pltpu.roll(north, 1, 1), above, below

    def speed(i, m):
        e, w, n, s_, a, c = [jnp.abs(v[0:32]) for v in cell(i)]
        v = e + w + n + s_ + a + c
        v = jnp.max(v.reshape(4, 8, N), axis=0)
        return jnp.maximum(m, jnp.maximum(jnp.maximum(v[:, :128], v[:, 128:256]),
                                          jnp.maximum(v[:, 256:384], v[:, 384:])))

    mx[0] = lax.fori_loop(HALO, HALO + ZL, speed, jnp.zeros((8, 128), F32))

    def copy_m(j, origin):
        return pltpu.make_async_remote_copy(
            src_ref=mx.at[0], dst_ref=mxh.at[origin], send_sem=ms.at[j], recv_sem=mq.at[j],
            device_id=dev(mate(j), d))

    def copy_n(j, origin):
        return pltpu.make_async_remote_copy(
            src_ref=mx.at[1], dst_ref=mxd.at[origin], send_sem=ns.at[j], recv_sem=nq.at[j],
            device_id=dev(h, lax.rem(d + j, ND)))

    def go_m(j, _):
        copy_m(j, h).start()
        return 0

    lax.fori_loop(1, NH, go_m, 0)
    def left_m(j, _):
        copy_m(j, h).wait_send()
        return 0
    drains["m"] = lambda: lax.fori_loop(1, NH, left_m, 0)
    mxh[h] = mx[0]

    def stencil(get, c_ref, i):
        c = c_ref[i]
        return (get(0) * c
                + get(1) * pltpu.roll(c, XE - 1, 0) + get(2) * pltpu.roll(c, 1, 0)
                + get(3) * pltpu.roll(c, N - 1, 1) + get(4) * pltpu.roll(c, 1, 1)
                + get(5) * c_ref[i + 1] + get(6) * c_ref[i - 1])

    def tendencies(m_ref, s_ref, i):
        get = lambda k: coef[k, i - 1]
        react = REACTION * m_ref[i] * s_ref[i]
        return (stencil(get, m_ref, i) + (react - VENT_INPUT * ev[...]),
                stencil(get, s_ref, i) + react)

    def prepare(i, _):
        e, w, n, s_, a, c = cell(i)
        pos, neg = (lambda v: jnp.maximum(v, 0.0)), (lambda v: jnp.minimum(v, 0.0))
        coef[0, i - 1] = (pos(e) - neg(w)) + (pos(n) - neg(s_)) + (pos(c) - neg(a))
        coef[1, i - 1] = neg(e)
        coef[2, i - 1] = -pos(w)
        coef[3, i - 1] = neg(n)
        coef[4, i - 1] = -pos(s_)
        coef[5, i - 1] = neg(c)
        coef[6, i - 1] = -pos(a)
        t_m, t_s = tendencies(em, es, i)
        tend[0, i - 1] = t_m
        tend[1, i - 1] = t_s
        return 0

    def bend(i, _):
        get = lambda k: coef[k, i - 1]
        curve[0, i - 2] = stencil(get, tend.at[0], i - 1)
        curve[1, i - 2] = stencil(get, tend.at[1], i - 1)
        return 0

    lax.fori_loop(HALO + 1, HALO + ZL - 1, prepare, 0)
    drains.pop("pr")()
    unpack_rows(0, ep, (0, 1, 6, 7))
    lax.fori_loop(1, HALO + 1, prepare, 0)
    lax.fori_loop(HALO + ZL - 1, ZE - 1, prepare, 0)
    lax.fori_loop(2, 9, bend, 0)

    def done_m(j, _):
        copy_m(j, lax.rem(h + NH - j, NH)).wait_recv()
        return 0

    lax.fori_loop(1, NH, done_m, 0)
    mx[1] = jnp.max(mxh[...], axis=0)

    def go_n(j, _):
        copy_n(j, d).start()
        return 0

    lax.fori_loop(1, ND, go_n, 0)
    def left_n(j, _):
        copy_n(j, d).wait_send()
        return 0
    drains["n"] = lambda: lax.fori_loop(1, ND, left_n, 0)
    mxd[d] = mx[1]

    lax.fori_loop(9, ZE - 2, bend, 0)

    def done_n(j, _):
        copy_n(j, lax.rem(d + ND - j, ND)).wait_recv()
        return 0

    lax.fori_loop(1, ND, done_n, 0)
    fastest = jnp.max(jnp.max(mxd[...], axis=0), axis=(0, 1), keepdims=True)
    dt = COURANT / (fastest + 1e-6)

    def first(i, _):
        m, s, t_m, t_s = em[i], es[i], tend[0, i - 1], tend[1, i - 1]
        m1, s1 = m - dt * t_m, s - dt * t_s
        more = REACTION * (m1 * s1) - REACTION * (m * s)
        em2[i] = m1 - dt * ((t_m + more) - dt * curve[0, i - 2])
        es2[i] = s1 - dt * ((t_s + more) - dt * curve[1, i - 2])
        return 0

    lax.fori_loop(2, ZE - 2, first, 0)

    def step(a, c, lo):
        def body(i, _):
            t_m, t_s = tendencies(a[0], a[1], i)
            c[0][i] = a[0][i] - dt * t_m
            c[1][i] = a[1][i] - dt * t_s
            return 0

        lax.fori_loop(lo, ZE - lo, body, 0)

    step((em2, es2), (em, es), 3)

    def last(i, _):
        t_m, t_s = tendencies(em, es, i)
        res_m[i - HALO] = (em[i] - dt * t_m)[0:32]
        res_s[i - HALO] = (es[i] - dt * t_s)[0:32]
        return 0

    for part in range(2):
        half = ZL // 2
        lax.fori_loop(HALO + half * part, HALO + half * (part + 1), last, 0)
        at = pl.ds(half * part, half)
        for k, (ref, out) in enumerate(((res_m, out_m), (res_s, out_s))):
            outs.append(pltpu.make_async_copy(ref.at[at], out.at[at], lsem.at[9 + 2 * part + k]))
            outs[-1].start()
    for f in drains.values():
        f()


def deliver(*refs):
    ins, outs, (buf, sem_in, sem_out) = refs[:3], refs[3:6], refs[6:]
    part = ZL // PARTS
    moves = []
    for k in range(3):
        for n in range(PARTS):
            at = pl.ds(n * part, part)
            moves.append((
                pltpu.make_async_copy(ins[k].at[at], buf.at[k, at], sem_in.at[k, n]),
                pltpu.make_async_copy(buf.at[k, at], outs[k].at[at], sem_out.at[k, n])))
    for a, _ in moves:
        a.start()
    for a, b in moves:
        a.wait()
        b.start()
    for _, b in moves:
        b.wait()


def local(source_field, methane, sulfate, layer_of_cell, perm_horizontal, perm_vertical, vent_mask):
    hi, lo, eig_x, eig_y = tables()
    smem = pl.BlockSpec(memory_space=pltpu.SMEM)
    hbm = pl.BlockSpec(memory_space=pl.ANY)
    field = jax.ShapeDtypeStruct((ZL, XL, N), F32)
    dma = pltpu.SemaphoreType.DMA
    ext = pltpu.VMEM((ZE, XE, N), F32)
    scratch = [
        pltpu.VMEM((ZL, XL, N), F32),
        pltpu.VMEM((XL, N), jnp.int32),
        pltpu.VMEM((N, N), BF16),
        pltpu.VMEM((N, N), BF16),
        pltpu.VMEM((16, N), F32),
        pltpu.VMEM((ZL, XL, N), F32),
        pltpu.VMEM((ZL, XL, N), F32),
        pltpu.VMEM((NQ, 16, ZL * XL), F32),
        pltpu.VMEM((NQ, 16, ZL * XL), F32),
        pltpu.VMEM((ZB * 16, N), BF16),
        pltpu.VMEM((ZB * 16, N), BF16),
        pltpu.VMEM((ZB, 16, N), F32),
        pltpu.VMEM((NQ, 16, ZL * XL), F32),
        pltpu.VMEM((NQ, 16, ZL * XL), F32),
        pltpu.VMEM((16, 128), F32),
        pltpu.VMEM((NZ, 16, N), F32),
        pltpu.VMEM((NZ, 16, N), F32),
        pltpu.VMEM((NX_CHIPS, 16, N), F32),
        pltpu.VMEM((NX_CHIPS, 16, N), F32),
        pltpu.VMEM((ZB, 16, N), F32),
        pltpu.VMEM((ZB, 16, N), F32),
        pltpu.VMEM((2, 16, N), F32),
        pltpu.VMEM((NX_CHIPS, 16, N), F32),
        ext, ext, ext, ext, ext,
        pltpu.VMEM((XE, N), F32),
        pltpu.VMEM((2, 8, N), F32),
        pltpu.VMEM((3, 2, ZL // 2, 8, N), F32),
        pltpu.VMEM((3, 2, ZE // 2, 8, N), F32),
        pltpu.VMEM((7, ZE - 2, XE, N), F32),
        pltpu.VMEM((2, ZE - 2, XE, N), F32),
        pltpu.VMEM((2, ZE - 4, XE, N), F32),
        pltpu.VMEM((2, 8, 128), F32),
        pltpu.VMEM((NH, 8, 128), F32),
        pltpu.VMEM((ND, 8, 128), F32),
        pltpu.SMEM((NZ + 1,), F32),
        pltpu.SMEM((NZ,), F32),
        dma((NQ,)), dma((NQ,)), dma((NX_CHIPS,)), dma((NX_CHIPS,)), dma((NQ,)), dma((NQ,)),
        dma((3, 12)), dma((3, 12)), dma((2,)), dma((2,)),
        dma((NH,)), dma((NH,)), dma((ND,)), dma((ND,)), dma((13,)),
    ]
    results = pl.pallas_call(
        kernel,
        out_shape=(field, field, field),
        in_specs=[hbm, hbm, hbm, smem, smem, smem, hbm, hbm, hbm, hbm, hbm],
        out_specs=(hbm, hbm, hbm),
        scratch_shapes=scratch,
        compiler_params=pltpu.CompilerParams(
            collective_id=0, has_side_effects=True, vmem_limit_bytes=60 * 1024 * 1024),
    )(source_field, methane, sulfate, layer_of_cell, perm_horizontal, perm_vertical, vent_mask,
      jnp.asarray(hi), jnp.asarray(lo), jnp.asarray(eig_x), jnp.asarray(eig_y))
    return pl.pallas_call(
        deliver,
        out_shape=(field, field, field),
        in_specs=[hbm] * 3,
        out_specs=(hbm,) * 3,
        scratch_shapes=[pltpu.VMEM((3, ZL, XL, N), F32), dma((3, PARTS)), dma((3, PARTS))],
    )(*results)


def solution(mesh):
    field = P("depth", "horiz", None)
    return jax.shard_map(
        local,
        mesh=mesh,
        in_specs=(field, field, field, P(), P(), P(), P("horiz", None)),
        out_specs=(field, field, field),
        check_vma=False,
    )
```

```python
import jax
import jax.numpy as jnp
import ml_dtypes
import numpy as np
from jax import lax
from jax.experimental import pallas as pl
from jax.experimental.pallas import tpu as pltpu
from jax.sharding import PartitionSpec as P

STEPS = 4
STORAGE = 0.004
COURANT = 0.5
REACTION = 4.0
VENT_INPUT = 4.0

NZ = 64
N = 512
NH = 16
ND = 8
ZL = 8
XL = 32
HALO = 4
ZE = ZL + 2 * HALO
XE = XL + 2 * HALO
NX_CHIPS = 4
ZB = NZ // NX_CHIPS
NQ = 2 * NH

PLANE = sorted(
    [(z, y, c) for z in range(4) for y in range(4) for c in range(2)][1:],
    key=lambda o: -(min(o[0], 4 - o[0]) + min(o[1], 4 - o[1])))

PARTS = 2

F32 = jnp.float32
BF16 = jnp.bfloat16


def tables():
    k = np.arange(N)
    angle = (k[:, None] * k[None, :] % N) * (2.0 * np.pi / N)
    cas = np.cos(angle) + np.sin(angle)
    hi = cas.astype(np.float32).astype(ml_dtypes.bfloat16)
    lo = (cas - hi.astype(np.float64)).astype(np.float32).astype(ml_dtypes.bfloat16)
    eig = (4.0 * np.sin(np.pi * k / N) ** 2).astype(np.float32)
    eig_x = np.broadcast_to(eig.reshape(1, N), (16, N)).copy()
    eig_y = np.broadcast_to(eig.reshape(NQ, 16, 1), (NQ, 16, 128)).copy()
    return hi, lo, eig_x, eig_y


def split(v):
    hi = v.astype(BF16)
    return hi, (v - hi.astype(F32)).astype(BF16)


def dot3(a, b, dims=((1,), (0,))):
    (ah, al), (bh, bl) = a, b
    d = lambda x, y: lax.dot_general(x, y, (dims, ((), ())), preferred_element_type=F32)
    return d(ah, bh) + (d(al, bh) + d(ah, bl))


def kernel(
    src_in, met, sul, layer, ph, pv, vent_in, hhi_in, hlo_in, eig_x_in, eig_y,
    out_p, out_m, out_s,
    src, vent, hhi, hlo, eig_x, res_m, res_s,
    y1, r1, ah, al, fz, w1, y4, ey,
    inv_d, inv_u, prod_d, prod_u, gd, pi, send_a, recv_a,
    ep, em, es, em2, es2, ev, vin, pack, xin, coef, tend, curve,
    mx, mxh, mxd, cpl, khs,
    s1, q1, s2, q2, s4, q4, hs, hq, vs, vq, ms, mq, ns, nq, lsem,
):
    h = lax.axis_index("horiz")
    d = lax.axis_index("depth")
    chip = lax.div(d, 2)
    core = lax.rem(d, 2)
    q = h * 2 + core

    drains = {}

    def dev(hh, dd):
        return {"horiz": hh, "depth": dd}

    def mate(j):
        return lax.rem(h + j, NH)

    hz, hy = lax.div(h, 4), lax.rem(h, 4)

    def fellow(j, sign=1):
        dz, dy, dc = PLANE[j]
        fh = lax.rem(hz + sign * dz + 4, 4) * 4 + lax.rem(hy + sign * dy + 4, 4)
        fc = lax.rem(core + dc, 2)
        return 2 * fh + fc, fh, fc

    def slot(oq):
        return lax.rem(oq, 2) * NH + lax.div(oq, 2)

    h_up, h_dn = lax.rem(h + 1, NH), lax.rem(h + NH - 1, NH)
    d_up, d_dn = lax.rem(d + 1, ND), lax.rem(d + ND - 1, ND)

    first_loads = [
        pltpu.make_async_copy(src_in, src, lsem.at[3]),
        pltpu.make_async_copy(hhi_in, hhi, lsem.at[4]),
        pltpu.make_async_copy(hlo_in, hlo, lsem.at[5]),
    ]
    for c in first_loads:
        c.start()

    barrier = pltpu.get_barrier_semaphore()

    for j in range(NQ - 1):
        _, fh, fc = fellow(j)
        pl.semaphore_signal(barrier, inc=1, device_id=dev(fh, 2 * chip + fc))

    def greet_d(j, _):
        pl.semaphore_signal(barrier, inc=1, device_id=dev(h, lax.rem(d + j, ND)))
        return 0

    lax.fori_loop(1, ND, greet_d, 0)
    for hh in (h_up, h_dn):
        for dd in (d_up, d_dn):
            pl.semaphore_signal(barrier, inc=1, device_id=dev(hh, dd))

    own_copies = [
        pltpu.make_async_copy(met, em.at[pl.ds(HALO, ZL), pl.ds(0, XL)], lsem.at[0]),
        pltpu.make_async_copy(sul, es.at[pl.ds(HALO, ZL), pl.ds(0, XL)], lsem.at[1]),
        pltpu.make_async_copy(eig_y.at[q], ey, lsem.at[2]),
        pltpu.make_async_copy(vent_in, vent, lsem.at[6]),
        pltpu.make_async_copy(eig_x_in, eig_x, lsem.at[7]),
    ]
    for c in own_copies:
        c.start()
    drains["own"] = lambda: [c.wait() for c in own_copies]

    for c in first_loads:
        c.wait()
    s = split(src[...].reshape(ZL * XL, N))
    for n in range(2):
        rows = (hhi[256 * n:256 * n + 256], hlo[256 * n:256 * n + 256])
        y1[16 * n:16 * n + 16] = dot3(rows, s, ((1,), (1,))).reshape(16, 16, ZL * XL)

    pl.semaphore_wait(barrier, (NQ - 1) + (ND - 1) + 4)

    def copy1(j, oq):
        pq, fh, fc = fellow(j)
        return pltpu.make_async_remote_copy(
            src_ref=y1.at[pq], dst_ref=r1.at[slot(oq)],
            send_sem=s1.at[j], recv_sem=q1.at[j], device_id=dev(fh, 2 * chip + fc))

    def go1():
        for j in range(NQ - 1):
            copy1(j, q).start()

    go1()
    def left1():
        for j in range(NQ - 1):
            copy1(j, q).wait_send()
    drains["1"] = left1

    def halo_copies(f, ref, dirs):
        own = pl.ds(0, XL)
        lo_p, hi_p = pack.at[f, 0], pack.at[f, 1]
        plan = (
            (ref.at[pl.ds(8, 4), own], ref.at[pl.ds(0, 4), own], h, d_up),
            (ref.at[pl.ds(4, 4), own], ref.at[pl.ds(12, 4), own], h, d_dn),
            (hi_p, xin.at[f, 0, pl.ds(2, 4)], h_up, d),
            (lo_p, xin.at[f, 1, pl.ds(2, 4)], h_dn, d),
            (hi_p.at[pl.ds(2, 2)], xin.at[f, 0, pl.ds(0, 2)], h_up, d_up),
            (hi_p.at[pl.ds(0, 2)], xin.at[f, 0, pl.ds(6, 2)], h_up, d_dn),
            (lo_p.at[pl.ds(2, 2)], xin.at[f, 1, pl.ds(0, 2)], h_dn, d_up),
            (lo_p.at[pl.ds(0, 2)], xin.at[f, 1, pl.ds(6, 2)], h_dn, d_dn),
            (ref.at[pl.ds(11, 1), own], ref.at[pl.ds(3, 1), own], h, d_up),
            (ref.at[pl.ds(4, 1), own], ref.at[pl.ds(12, 1), own], h, d_dn),
            (ref.at[pl.ds(8, 3), own], ref.at[pl.ds(0, 3), own], h, d_up),
            (ref.at[pl.ds(5, 3), own], ref.at[pl.ds(13, 3), own], h, d_dn),
        )
        return [
            pltpu.make_async_remote_copy(
                src_ref=plan[i][0], dst_ref=plan[i][1], send_sem=hs.at[f, i], recv_sem=hq.at[f, i],
                device_id=dev(plan[i][2], plan[i][3]))
            for i in dirs
        ]

    sub8 = lax.broadcasted_iota(jnp.int32, (8, N), 0)

    def pack_rows(f, ref):
        for zz in range(ZL // 2):
            even, odd = ref[HALO + 2 * zz], ref[HALO + 2 * zz + 1]
            pack[f, 0, zz] = jnp.where(sub8 < 4, even[0:8], pltpu.roll(odd[0:8], 4, 0))
            pack[f, 1, zz] = jnp.where(sub8 >= 4, even[24:32], pltpu.roll(odd[24:32], 4, 0))

    def unpack_rows(f, ref, pairs=range(ZE // 2)):
        for zz in pairs:
            lower, upper = xin[f, 0, zz], xin[f, 1, zz]
            ref[2 * zz, XL:XE] = jnp.where(sub8 < 4, upper, lower)
            ref[2 * zz + 1, XL:XE] = pltpu.roll(jnp.where(sub8 < 4, lower, upper), 4, 0)

    drains.pop("own")()
    conc = ((1, em), (2, es))
    for f, ref in conc:
        for c in halo_copies(f, ref, (0, 1)):
            c.start()
    drains["c01"] = lambda: [c.wait() for f, ref in conc for c in halo_copies(f, ref, (0, 1))]
    for f, ref in conc:
        pack_rows(f, ref)
    ev[0:32] = vent[...].astype(F32)
    vent_copies = [
        pltpu.make_async_remote_copy(
            src_ref=ev.at[pl.ds(24, 8)], dst_ref=vin.at[0],
            send_sem=vs.at[0], recv_sem=vq.at[0], device_id=dev(h_up, d)),
        pltpu.make_async_remote_copy(
            src_ref=ev.at[pl.ds(0, 8)], dst_ref=vin.at[1],
            send_sem=vs.at[1], recv_sem=vq.at[1], device_id=dev(h_dn, d)),
    ]

    def table(z, _):
        khs[z] = ph[layer[z]]
        return 0

    lax.fori_loop(0, NZ, table, 0)
    cpl[0] = 0.0
    cpl[NZ] = 0.0

    def face(i, _):
        a, c = pv[layer[i - 1]], pv[layer[i]]
        cpl[i] = 2.0 * a * c / (a + c)
        return 0

    lax.fori_loop(1, NZ, face, 0)

    lam = eig_x[...] + jnp.concatenate([ey[...]] * 4, axis=1)
    blank = jnp.zeros((16, N), F32)
    state = (blank, blank)
    for j in range(NX_CHIPS):
        def factor(i, carry, j=j):
            rd, ru, bd, bu = carry
            z, y = ZB * j + i, NZ - 1 - ZB * j - i
            cu, cd = cpl[z], cpl[z + 1]
            v = 1.0 / ((cu + cd + khs[z] * lam + STORAGE) - cu * rd)
            inv_d[z] = v
            rd, bd = cd * v, bd * (cu * v)
            cu, cd = cpl[y], cpl[y + 1]
            v = 1.0 / ((cu + cd + khs[y] * lam + STORAGE) - cd * ru)
            inv_u[y] = v
            ru, bu = cu * v, bu * (cd * v)
            return rd, ru, bd, bu

        rd, ru, bd, bu = lax.fori_loop(0, ZB, factor, state + (blank + 1.0, blank + 1.0))
        state = (rd, ru)
        prod_d[j] = bd
        prod_u[NX_CHIPS - 1 - j] = bu
    base = ZB * chip

    def product(i, v):
        v = v * (cpl[base + i] * inv_d[base + i])
        pi[i] = v
        return v

    lax.fori_loop(0, ZB, product, blank + 1.0)
    r_last = cpl[base + ZB] * inv_d[base + ZB - 1]
    r_next = cpl[base + ZB] * inv_u[jnp.minimum(base + ZB, NZ - 1)]
    join = 1.0 / (1.0 - r_last * r_next)

    r1[slot(q)] = y1[q]

    for j in range(NQ - 1):
        copy1(j, fellow(j, -1)[0]).wait_recv()
    for f, ref in conc:
        for c in halo_copies(f, ref, range(2, 8)):
            c.start()
    for c in vent_copies:
        c.start()
    drains["c28"] = lambda: [c.wait() for c in vent_copies + [c for f, ref in conc for c in halo_copies(f, ref, range(2, 8))]]

    group = lax.broadcasted_iota(jnp.int32, (16, 128), 1) // 32

    def regroup(v):
        lower, even = group < 2, lax.rem(group, 2) == 0
        p = [jnp.where(lower, v[i], pltpu.roll(v[i + 2], 64, 1)) for i in range(2)]
        r = [jnp.where(lower, pltpu.roll(v[i], 64, 1), v[i + 2]) for i in range(2)]
        out = []
        for a, b in (p, r):
            out.append(jnp.where(even, a, pltpu.roll(b, 32, 1)))
            out.append(jnp.where(even, pltpu.roll(a, 96, 1), b))
        return out

    for c in range(2):
        for g in range(2):
            for t in range(4):
                v = regroup([r1[NH * c + 4 * t + i, :, 128 * g:128 * g + 128] for i in range(4)])
                for i in range(4):
                    row = 16 * (8 * c + 4 * g + i)
                    hi, lo = split(v[i])
                    ah[row:row + 16, 128 * t:128 * t + 128] = hi
                    al[row:row + 16, 128 * t:128 * t + 128] = lo
    for n in range(2):
        cols = (hhi[:, 256 * n:256 * n + 256], hlo[:, 256 * n:256 * n + 256])
        o = dot3((ah[...], al[...]), cols)
        fz[:, :, 256 * n:256 * n + 256] = (o * (1.0 / (N * N))).reshape(ZB, 16, 256)

    def down(i, v):
        k = inv_d[base + i]
        v = fz[i] * k + (cpl[base + i] * k) * v
        gd[i] = v
        return v

    def upward(n, v):
        i = ZB - 1 - n
        k = inv_u[base + i]
        return fz[i] * k + (cpl[base + i + 1] * k) * v

    send_a[0] = lax.fori_loop(0, ZB, down, blank, unroll=4)
    send_a[1] = lax.fori_loop(0, ZB, upward, blank, unroll=4)

    def copy2(j, origin):
        to = lax.rem(chip + j, NX_CHIPS)
        return pltpu.make_async_remote_copy(
            src_ref=send_a.at[jnp.where(to > chip, 0, 1)], dst_ref=recv_a.at[origin],
            send_sem=s2.at[j], recv_sem=q2.at[j], device_id=dev(h, 2 * to + core))

    def go2(j, _):
        copy2(j, chip).start()
        return 0

    lax.fori_loop(1, NX_CHIPS, go2, 0)

    def left2(j, _):
        copy2(j, chip).wait_send()
        return 0

    drains["2"] = lambda: lax.fori_loop(1, NX_CHIPS, left2, 0)
    recv_a[chip] = blank

    def done2(j, _):
        copy2(j, lax.rem(chip + NX_CHIPS - j, NX_CHIPS)).wait_recv()
        return 0

    lax.fori_loop(1, NX_CHIPS, done2, 0)
    from_top, from_bottom = blank, blank
    for j in range(NX_CHIPS - 1):
        from_top = jnp.where(j < chip, recv_a[j] + prod_d[j] * from_top, from_top)
        k = NX_CHIPS - 1 - j
        from_bottom = jnp.where(k > chip, recv_a[k] + prod_u[k] * from_bottom, from_bottom)

    def solved(i, p):
        row = pl.ds(pl.multiple_of(16 * i, 16), 16)
        hi, lo = split(p)
        ah[row, :] = hi
        al[row, :] = lo

    p = (gd[ZB - 1] + pi[ZB - 1] * from_top + r_last * from_bottom) * join
    solved(ZB - 1, p)

    def up(n, p):
        i = ZB - 2 - n
        p = gd[i] + pi[i] * from_top + (cpl[base + i + 1] * inv_d[base + i]) * p
        solved(i, p)
        return p

    lax.fori_loop(0, ZB - 1, up, p)
    for n in range(2):
        cols = (hhi[:, 256 * n:256 * n + 256], hlo[:, 256 * n:256 * n + 256])
        fz[:, :, 256 * n:256 * n + 256] = dot3((ah[...], al[...]), cols).reshape(ZB, 16, 256)
    for c in range(2):
        for g in range(2):
            for t in range(4):
                v = regroup([fz[8 * c + 4 * g + i, :, 128 * t:128 * t + 128] for i in range(4)])
                for i in range(4):
                    w1[NH * c + 4 * t + i, :, 128 * g:128 * g + 128] = v[i]

    def copy4(j, oq):
        pq, fh, fc = fellow(j)
        return pltpu.make_async_remote_copy(
            src_ref=w1.at[slot(pq)], dst_ref=y4.at[oq],
            send_sem=s4.at[j], recv_sem=q4.at[j], device_id=dev(fh, 2 * chip + fc))

    def go4():
        for j in range(NQ - 1):
            copy4(j, q).start()

    go4()

    def left4():
        for j in range(NQ - 1):
            copy4(j, q).wait_send()

    drains["4"] = left4
    y4[q] = w1[slot(q)]

    del drains["c01"], drains["c28"]
    for f, ref in conc:
        for c in halo_copies(f, ref, range(8)):
            c.wait()
        unpack_rows(f, ref)
    for c in vent_copies:
        c.wait()
    ev[XL:XE] = jnp.where(sub8 < 4, vin[1], vin[0])

    for j in range(NQ - 1):
        copy4(j, fellow(j, -1)[0]).wait_recv()

    s = split(y4[...].reshape(N, ZL * XL).T)
    for n in range(2):
        o = dot3(s, (hhi[:, 256 * n:256 * n + 256], hlo[:, 256 * n:256 * n + 256]))
        ep[HALO:HALO + ZL, 0:32, 256 * n:256 * n + 256] = o.reshape(ZL, XL, 256)
    outs = [pltpu.make_async_copy(ep.at[pl.ds(HALO, ZL), pl.ds(0, XL)], out_p, lsem.at[8])]
    outs[0].start()
    drains["out"] = lambda: [c.wait() for c in outs]

    near = halo_copies(0, ep, (8, 9, 2, 3))
    rest = halo_copies(0, ep, (10, 11, 4, 5, 6, 7))
    for c in near[:2]:
        c.start()
    pack_rows(0, ep)
    for c in near[2:] + rest:
        c.start()
    drains["p"] = lambda: [c.wait_send() for c in near + rest]
    drains["pr"] = lambda: [c.wait_recv() for c in rest]
    for c in near:
        c.wait_recv()
    unpack_rows(0, ep, (2, 3, 4, 5))

    def cell(i):
        gz = lax.rem(d * ZL + i + (NZ - HALO), NZ)
        kh, cu, cd = khs[gz], cpl[gz], cpl[gz + 1]
        p = ep[i]
        east = -kh * (pltpu.roll(p, XE - 1, 0) - p)
        north = -kh * (pltpu.roll(p, N - 1, 1) - p)
        above = -cu * (p - ep[i - 1])
        below = -cd * (ep[i + 1] - p)
        return east, pltpu.roll(east, 1, 0), north, pltpu.roll(north, 1, 1), above, below

    def speed(i, m):
        e, w, n, s_, a, c = [jnp.abs(v[0:32]) for v in cell(i)]
        v = e + w + n + s_ + a + c
        v = jnp.max(v.reshape(4, 8, N), axis=0)
        return jnp.maximum(m, jnp.maximum(jnp.maximum(v[:, :128], v[:, 128:256]),
                                          jnp.maximum(v[:, 256:384], v[:, 384:])))

    mx[0] = lax.fori_loop(HALO, HALO + ZL, speed, jnp.zeros((8, 128), F32))

    def copy_m(j, origin):
        return pltpu.make_async_remote_copy(
            src_ref=mx.at[0], dst_ref=mxh.at[origin], send_sem=ms.at[j], recv_sem=mq.at[j],
            device_id=dev(mate(j), d))

    def copy_n(j, origin):
        return pltpu.make_async_remote_copy(
            src_ref=mx.at[1], dst_ref=mxd.at[origin], send_sem=ns.at[j], recv_sem=nq.at[j],
            device_id=dev(h, lax.rem(d + j, ND)))

    def go_m(j, _):
        copy_m(j, h).start()
        return 0

    lax.fori_loop(1, NH, go_m, 0)
    def left_m(j, _):
        copy_m(j, h).wait_send()
        return 0
    drains["m"] = lambda: lax.fori_loop(1, NH, left_m, 0)
    mxh[h] = mx[0]

    def stencil(get, c_ref, i):
        c = c_ref[i]
        return (get(0) * c
                + get(1) * pltpu.roll(c, XE - 1, 0) + get(2) * pltpu.roll(c, 1, 0)
                + get(3) * pltpu.roll(c, N - 1, 1) + get(4) * pltpu.roll(c, 1, 1)
                + get(5) * c_ref[i + 1] + get(6) * c_ref[i - 1])

    def tendencies(m_ref, s_ref, i):
        get = lambda k: coef[k, i - 1]
        react = REACTION * m_ref[i] * s_ref[i]
        return (stencil(get, m_ref, i) + (react - VENT_INPUT * ev[...]),
                stencil(get, s_ref, i) + react)

    def prepare(i, _):
        e, w, n, s_, a, c = cell(i)
        pos, neg = (lambda v: jnp.maximum(v, 0.0)), (lambda v: jnp.minimum(v, 0.0))
        coef[0, i - 1] = (pos(e) - neg(w)) + (pos(n) - neg(s_)) + (pos(c) - neg(a))
        coef[1, i - 1] = neg(e)
        coef[2, i - 1] = -pos(w)
        coef[3, i - 1] = neg(n)
        coef[4, i - 1] = -pos(s_)
        coef[5, i - 1] = neg(c)
        coef[6, i - 1] = -pos(a)
        t_m, t_s = tendencies(em, es, i)
        tend[0, i - 1] = t_m
        tend[1, i - 1] = t_s
        return 0

    def bend(i, _):
        get = lambda k: coef[k, i - 1]
        curve[0, i - 2] = stencil(get, tend.at[0], i - 1)
        curve[1, i - 2] = stencil(get, tend.at[1], i - 1)
        return 0

    lax.fori_loop(HALO + 1, HALO + ZL - 1, prepare, 0)
    drains.pop("pr")()
    unpack_rows(0, ep, (0, 1, 6, 7))
    lax.fori_loop(1, HALO + 1, prepare, 0)
    lax.fori_loop(HALO + ZL - 1, ZE - 1, prepare, 0)

    def done_m(j, _):
        copy_m(j, lax.rem(h + NH - j, NH)).wait_recv()
        return 0

    lax.fori_loop(1, NH, done_m, 0)
    mx[1] = jnp.max(mxh[...], axis=0)

    def go_n(j, _):
        copy_n(j, d).start()
        return 0

    lax.fori_loop(1, ND, go_n, 0)
    def left_n(j, _):
        copy_n(j, d).wait_send()
        return 0
    drains["n"] = lambda: lax.fori_loop(1, ND, left_n, 0)
    mxd[d] = mx[1]

    lax.fori_loop(2, ZE - 2, bend, 0)

    def done_n(j, _):
        copy_n(j, lax.rem(d + ND - j, ND)).wait_recv()
        return 0

    lax.fori_loop(1, ND, done_n, 0)
    fastest = jnp.max(jnp.max(mxd[...], axis=0), axis=(0, 1), keepdims=True)
    dt = COURANT / (fastest + 1e-6)

    def first(i, _):
        m, s, t_m, t_s = em[i], es[i], tend[0, i - 1], tend[1, i - 1]
        m1, s1 = m - dt * t_m, s - dt * t_s
        more = REACTION * (m1 * s1) - REACTION * (m * s)
        em2[i] = m1 - dt * ((t_m + more) - dt * curve[0, i - 2])
        es2[i] = s1 - dt * ((t_s + more) - dt * curve[1, i - 2])
        return 0

    lax.fori_loop(2, ZE - 2, first, 0)

    def step(a, c, lo):
        def body(i, _):
            t_m, t_s = tendencies(a[0], a[1], i)
            c[0][i] = a[0][i] - dt * t_m
            c[1][i] = a[1][i] - dt * t_s
            return 0

        lax.fori_loop(lo, ZE - lo, body, 0)

    step((em2, es2), (em, es), 3)

    def last(i, _):
        t_m, t_s = tendencies(em, es, i)
        res_m[i - HALO] = (em[i] - dt * t_m)[0:32]
        res_s[i - HALO] = (es[i] - dt * t_s)[0:32]
        return 0

    for part in range(2):
        half = ZL // 2
        lax.fori_loop(HALO + half * part, HALO + half * (part + 1), last, 0)
        at = pl.ds(half * part, half)
        for k, (ref, out) in enumerate(((res_m, out_m), (res_s, out_s))):
            outs.append(pltpu.make_async_copy(ref.at[at], out.at[at], lsem.at[9 + 2 * part + k]))
            outs[-1].start()
    for f in drains.values():
        f()


def deliver(*refs):
    ins, outs, (buf, sem_in, sem_out) = refs[:3], refs[3:6], refs[6:]
    part = ZL // PARTS
    moves = []
    for k in range(3):
        for n in range(PARTS):
            at = pl.ds(n * part, part)
            moves.append((
                pltpu.make_async_copy(ins[k].at[at], buf.at[k, at], sem_in.at[k, n]),
                pltpu.make_async_copy(buf.at[k, at], outs[k].at[at], sem_out.at[k, n])))
    for a, _ in moves:
        a.start()
    for a, b in moves:
        a.wait()
        b.start()
    for _, b in moves:
        b.wait()


def local(source_field, methane, sulfate, layer_of_cell, perm_horizontal, perm_vertical, vent_mask):
    hi, lo, eig_x, eig_y = tables()
    smem = pl.BlockSpec(memory_space=pltpu.SMEM)
    hbm = pl.BlockSpec(memory_space=pl.ANY)
    field = jax.ShapeDtypeStruct((ZL, XL, N), F32)
    dma = pltpu.SemaphoreType.DMA
    ext = pltpu.VMEM((ZE, XE, N), F32)
    scratch = [
        pltpu.VMEM((ZL, XL, N), F32),
        pltpu.VMEM((XL, N), jnp.int32),
        pltpu.VMEM((N, N), BF16),
        pltpu.VMEM((N, N), BF16),
        pltpu.VMEM((16, N), F32),
        pltpu.VMEM((ZL, XL, N), F32),
        pltpu.VMEM((ZL, XL, N), F32),
        pltpu.VMEM((NQ, 16, ZL * XL), F32),
        pltpu.VMEM((NQ, 16, ZL * XL), F32),
        pltpu.VMEM((ZB * 16, N), BF16),
        pltpu.VMEM((ZB * 16, N), BF16),
        pltpu.VMEM((ZB, 16, N), F32),
        pltpu.VMEM((NQ, 16, ZL * XL), F32),
        pltpu.VMEM((NQ, 16, ZL * XL), F32),
        pltpu.VMEM((16, 128), F32),
        pltpu.VMEM((NZ, 16, N), F32),
        pltpu.VMEM((NZ, 16, N), F32),
        pltpu.VMEM((NX_CHIPS, 16, N), F32),
        pltpu.VMEM((NX_CHIPS, 16, N), F32),
        pltpu.VMEM((ZB, 16, N), F32),
        pltpu.VMEM((ZB, 16, N), F32),
        pltpu.VMEM((2, 16, N), F32),
        pltpu.VMEM((NX_CHIPS, 16, N), F32),
        ext, ext, ext, ext, ext,
        pltpu.VMEM((XE, N), F32),
        pltpu.VMEM((2, 8, N), F32),
        pltpu.VMEM((3, 2, ZL // 2, 8, N), F32),
        pltpu.VMEM((3, 2, ZE // 2, 8, N), F32),
        pltpu.VMEM((7, ZE - 2, XE, N), F32),
        pltpu.VMEM((2, ZE - 2, XE, N), F32),
        pltpu.VMEM((2, ZE - 4, XE, N), F32),
        pltpu.VMEM((2, 8, 128), F32),
        pltpu.VMEM((NH, 8, 128), F32),
        pltpu.VMEM((ND, 8, 128), F32),
        pltpu.SMEM((NZ + 1,), F32),
        pltpu.SMEM((NZ,), F32),
        dma((NQ,)), dma((NQ,)), dma((NX_CHIPS,)), dma((NX_CHIPS,)), dma((NQ,)), dma((NQ,)),
        dma((3, 12)), dma((3, 12)), dma((2,)), dma((2,)),
        dma((NH,)), dma((NH,)), dma((ND,)), dma((ND,)), dma((13,)),
    ]
    results = pl.pallas_call(
        kernel,
        out_shape=(field, field, field),
        in_specs=[hbm, hbm, hbm, smem, smem, smem, hbm, hbm, hbm, hbm, hbm],
        out_specs=(hbm, hbm, hbm),
        scratch_shapes=scratch,
        compiler_params=pltpu.CompilerParams(
            collective_id=0, has_side_effects=True, vmem_limit_bytes=60 * 1024 * 1024),
    )(source_field, methane, sulfate, layer_of_cell, perm_horizontal, perm_vertical, vent_mask,
      jnp.asarray(hi), jnp.asarray(lo), jnp.asarray(eig_x), jnp.asarray(eig_y))
    return pl.pallas_call(
        deliver,
        out_shape=(field, field, field),
        in_specs=[hbm] * 3,
        out_specs=(hbm,) * 3,
        scratch_shapes=[pltpu.VMEM((3, ZL, XL, N), F32), dma((3, PARTS)), dma((3, PARTS))],
    )(*results)


def solution(mesh):
    field = P("depth", "horiz", None)
    return jax.shard_map(
        local,
        mesh=mesh,
        in_specs=(field, field, field, P(), P(), P(), P("horiz", None)),
        out_specs=(field, field, field),
        check_vma=False,
    )
```

```python
import jax
import jax.numpy as jnp
import ml_dtypes
import numpy as np
from jax import lax
from jax.experimental import pallas as pl
from jax.experimental.pallas import tpu as pltpu
from jax.sharding import PartitionSpec as P

STEPS = 4
STORAGE = 0.004
COURANT = 0.5
REACTION = 4.0
VENT_INPUT = 4.0

NZ = 64
N = 512
NH = 16
ND = 8
ZL = 8
XL = 32
HALO = 4
ZE = ZL + 2 * HALO
XE = XL + 2 * HALO
NX_CHIPS = 4
ZB = NZ // NX_CHIPS
NQ = 2 * NH

PLANE = sorted(
    [(z, y, c) for z in range(4) for y in range(4) for c in range(2)][1:],
    key=lambda o: -(min(o[0], 4 - o[0]) + min(o[1], 4 - o[1])))

PARTS = 2

F32 = jnp.float32
BF16 = jnp.bfloat16


def tables():
    k = np.arange(N)
    angle = (k[:, None] * k[None, :] % N) * (2.0 * np.pi / N)
    cas = np.cos(angle) + np.sin(angle)
    hi = cas.astype(np.float32).astype(ml_dtypes.bfloat16)
    lo = (cas - hi.astype(np.float64)).astype(np.float32).astype(ml_dtypes.bfloat16)
    eig = (4.0 * np.sin(np.pi * k / N) ** 2).astype(np.float32)
    eig_x = np.broadcast_to(eig.reshape(1, N), (16, N)).copy()
    eig_y = np.broadcast_to(eig.reshape(NQ, 16, 1), (NQ, 16, 128)).copy()
    return hi, lo, eig_x, eig_y


def split(v):
    hi = v.astype(BF16)
    return hi, (v - hi.astype(F32)).astype(BF16)


def dot3(a, b, dims=((1,), (0,))):
    (ah, al), (bh, bl) = a, b
    d = lambda x, y: lax.dot_general(x, y, (dims, ((), ())), preferred_element_type=F32)
    return d(ah, bh) + (d(al, bh) + d(ah, bl))


def kernel(
    src_in, met, sul, layer_in, ph_in, pv_in, vent_in, hhi_in, hlo_in, eig_x_in, eig_y,
    out_p, out_m, out_s,
    src, vent, hhi, hlo, eig_x, res_m, res_s, layer, ph, pv,
    y1, r1, ah, al, fz, w1, y4, ey,
    inv_d, inv_u, prod_d, prod_u, gd, pi, send_a, recv_a,
    ep, em, es, em2, es2, ev, vin, pack, xin, coef, tend, curve,
    mx, mxh, mxd, cpl, khs,
    s1, q1, s2, q2, s4, q4, hs, hq, vs, vq, ms, mq, ns, nq, lsem,
):
    h = lax.axis_index("horiz")
    d = lax.axis_index("depth")
    chip = lax.div(d, 2)
    core = lax.rem(d, 2)
    q = h * 2 + core

    drains = {}

    def dev(hh, dd):
        return {"horiz": hh, "depth": dd}

    def mate(j):
        return lax.rem(h + j, NH)

    hz, hy = lax.div(h, 4), lax.rem(h, 4)

    def fellow(j, sign=1):
        dz, dy, dc = PLANE[j]
        fh = lax.rem(hz + sign * dz + 4, 4) * 4 + lax.rem(hy + sign * dy + 4, 4)
        fc = lax.rem(core + dc, 2)
        return 2 * fh + fc, fh, fc

    def slot(oq):
        return lax.rem(oq, 2) * NH + lax.div(oq, 2)

    h_up, h_dn = lax.rem(h + 1, NH), lax.rem(h + NH - 1, NH)
    d_up, d_dn = lax.rem(d + 1, ND), lax.rem(d + ND - 1, ND)

    first_loads = [
        pltpu.make_async_copy(src_in, src, lsem.at[3]),
        pltpu.make_async_copy(hhi_in, hhi, lsem.at[4]),
        pltpu.make_async_copy(hlo_in, hlo, lsem.at[5]),
    ]
    for c in first_loads:
        c.start()

    barrier = pltpu.get_barrier_semaphore()

    for j in range(NQ - 1):
        _, fh, fc = fellow(j)
        pl.semaphore_signal(barrier, inc=1, device_id=dev(fh, 2 * chip + fc))

    def greet_d(j, _):
        pl.semaphore_signal(barrier, inc=1, device_id=dev(h, lax.rem(d + j, ND)))
        return 0

    lax.fori_loop(1, ND, greet_d, 0)
    for hh in (h_up, h_dn):
        for dd in (d_up, d_dn):
            pl.semaphore_signal(barrier, inc=1, device_id=dev(hh, dd))

    own_copies = [
        pltpu.make_async_copy(met, em.at[pl.ds(HALO, ZL), pl.ds(0, XL)], lsem.at[0]),
        pltpu.make_async_copy(sul, es.at[pl.ds(HALO, ZL), pl.ds(0, XL)], lsem.at[1]),
        pltpu.make_async_copy(eig_y.at[q], ey, lsem.at[2]),
        pltpu.make_async_copy(vent_in, vent, lsem.at[6]),
        pltpu.make_async_copy(eig_x_in, eig_x, lsem.at[7]),
        pltpu.make_async_copy(layer_in, layer, lsem.at[13]),
        pltpu.make_async_copy(ph_in, ph, lsem.at[14]),
        pltpu.make_async_copy(pv_in, pv, lsem.at[15]),
    ]
    for c in own_copies:
        c.start()
    drains["own"] = lambda: [c.wait() for c in own_copies]

    for c in first_loads:
        c.wait()
    s = split(src[...].reshape(ZL * XL, N))
    for n in range(2):
        rows = (hhi[256 * n:256 * n + 256], hlo[256 * n:256 * n + 256])
        y1[16 * n:16 * n + 16] = dot3(rows, s, ((1,), (1,))).reshape(16, 16, ZL * XL)

    pl.semaphore_wait(barrier, (NQ - 1) + (ND - 1) + 4)

    def copy1(j, oq):
        pq, fh, fc = fellow(j)
        return pltpu.make_async_remote_copy(
            src_ref=y1.at[pq], dst_ref=r1.at[slot(oq)],
            send_sem=s1.at[j], recv_sem=q1.at[j], device_id=dev(fh, 2 * chip + fc))

    def go1():
        for j in range(NQ - 1):
            copy1(j, q).start()

    go1()
    def left1():
        for j in range(NQ - 1):
            copy1(j, q).wait_send()
    drains["1"] = left1

    def halo_copies(f, ref, dirs):
        own = pl.ds(0, XL)
        lo_p, hi_p = pack.at[f, 0], pack.at[f, 1]
        plan = (
            (ref.at[pl.ds(8, 4), own], ref.at[pl.ds(0, 4), own], h, d_up),
            (ref.at[pl.ds(4, 4), own], ref.at[pl.ds(12, 4), own], h, d_dn),
            (hi_p, xin.at[f, 0, pl.ds(2, 4)], h_up, d),
            (lo_p, xin.at[f, 1, pl.ds(2, 4)], h_dn, d),
            (hi_p.at[pl.ds(2, 2)], xin.at[f, 0, pl.ds(0, 2)], h_up, d_up),
            (hi_p.at[pl.ds(0, 2)], xin.at[f, 0, pl.ds(6, 2)], h_up, d_dn),
            (lo_p.at[pl.ds(2, 2)], xin.at[f, 1, pl.ds(0, 2)], h_dn, d_up),
            (lo_p.at[pl.ds(0, 2)], xin.at[f, 1, pl.ds(6, 2)], h_dn, d_dn),
            (ref.at[pl.ds(11, 1), own], ref.at[pl.ds(3, 1), own], h, d_up),
            (ref.at[pl.ds(4, 1), own], ref.at[pl.ds(12, 1), own], h, d_dn),
            (ref.at[pl.ds(8, 3), own], ref.at[pl.ds(0, 3), own], h, d_up),
            (ref.at[pl.ds(5, 3), own], ref.at[pl.ds(13, 3), own], h, d_dn),
        )
        return [
            pltpu.make_async_remote_copy(
                src_ref=plan[i][0], dst_ref=plan[i][1], send_sem=hs.at[f, i], recv_sem=hq.at[f, i],
                device_id=dev(plan[i][2], plan[i][3]))
            for i in dirs
        ]

    sub8 = lax.broadcasted_iota(jnp.int32, (8, N), 0)

    def pack_rows(f, ref):
        for zz in range(ZL // 2):
            even, odd = ref[HALO + 2 * zz], ref[HALO + 2 * zz + 1]
            pack[f, 0, zz] = jnp.where(sub8 < 4, even[0:8], pltpu.roll(odd[0:8], 4, 0))
            pack[f, 1, zz] = jnp.where(sub8 >= 4, even[24:32], pltpu.roll(odd[24:32], 4, 0))

    def unpack_rows(f, ref, pairs=range(ZE // 2)):
        for zz in pairs:
            lower, upper = xin[f, 0, zz], xin[f, 1, zz]
            ref[2 * zz, XL:XE] = jnp.where(sub8 < 4, upper, lower)
            ref[2 * zz + 1, XL:XE] = pltpu.roll(jnp.where(sub8 < 4, lower, upper), 4, 0)

    drains.pop("own")()
    conc = ((1, em), (2, es))
    for f, ref in conc:
        for c in halo_copies(f, ref, (0, 1)):
            c.start()
    drains["c01"] = lambda: [c.wait() for f, ref in conc for c in halo_copies(f, ref, (0, 1))]
    for f, ref in conc:
        pack_rows(f, ref)
    ev[0:32] = vent[...].astype(F32)
    vent_copies = [
        pltpu.make_async_remote_copy(
            src_ref=ev.at[pl.ds(24, 8)], dst_ref=vin.at[0],
            send_sem=vs.at[0], recv_sem=vq.at[0], device_id=dev(h_up, d)),
        pltpu.make_async_remote_copy(
            src_ref=ev.at[pl.ds(0, 8)], dst_ref=vin.at[1],
            send_sem=vs.at[1], recv_sem=vq.at[1], device_id=dev(h_dn, d)),
    ]

    def table(z, _):
        khs[z] = ph[layer[z]]
        return 0

    lax.fori_loop(0, NZ, table, 0)
    cpl[0] = 0.0
    cpl[NZ] = 0.0

    def face(i, _):
        a, c = pv[layer[i - 1]], pv[layer[i]]
        cpl[i] = 2.0 * a * c / (a + c)
        return 0

    lax.fori_loop(1, NZ, face, 0)

    lam = eig_x[...] + jnp.concatenate([ey[...]] * 4, axis=1)
    blank = jnp.zeros((16, N), F32)
    state = (blank, blank)
    for j in range(NX_CHIPS):
        def factor(i, carry, j=j):
            rd, ru, bd, bu = carry
            z, y = ZB * j + i, NZ - 1 - ZB * j - i
            cu, cd = cpl[z], cpl[z + 1]
            v = 1.0 / ((cu + cd + khs[z] * lam + STORAGE) - cu * rd)
            inv_d[z] = v
            rd, bd = cd * v, bd * (cu * v)
            cu, cd = cpl[y], cpl[y + 1]
            v = 1.0 / ((cu + cd + khs[y] * lam + STORAGE) - cd * ru)
            inv_u[y] = v
            ru, bu = cu * v, bu * (cd * v)
            return rd, ru, bd, bu

        rd, ru, bd, bu = lax.fori_loop(0, ZB, factor, state + (blank + 1.0, blank + 1.0))
        state = (rd, ru)
        prod_d[j] = bd
        prod_u[NX_CHIPS - 1 - j] = bu
    base = ZB * chip

    def product(i, v):
        v = v * (cpl[base + i] * inv_d[base + i])
        pi[i] = v
        return v

    lax.fori_loop(0, ZB, product, blank + 1.0)
    r_last = cpl[base + ZB] * inv_d[base + ZB - 1]
    r_next = cpl[base + ZB] * inv_u[jnp.minimum(base + ZB, NZ - 1)]
    join = 1.0 / (1.0 - r_last * r_next)

    r1[slot(q)] = y1[q]

    for j in range(8):
        copy1(j, fellow(j, -1)[0]).wait_recv()
    for f, ref in conc:
        for c in halo_copies(f, ref, range(2, 8)):
            c.start()
    for c in vent_copies:
        c.start()
    drains["c28"] = lambda: [c.wait() for c in vent_copies + [c for f, ref in conc for c in halo_copies(f, ref, range(2, 8))]]

    for j in range(8, NQ - 1):
        copy1(j, fellow(j, -1)[0]).wait_recv()
    group = lax.broadcasted_iota(jnp.int32, (16, 128), 1) // 32

    def regroup(v):
        lower, even = group < 2, lax.rem(group, 2) == 0
        p = [jnp.where(lower, v[i], pltpu.roll(v[i + 2], 64, 1)) for i in range(2)]
        r = [jnp.where(lower, pltpu.roll(v[i], 64, 1), v[i + 2]) for i in range(2)]
        out = []
        for a, b in (p, r):
            out.append(jnp.where(even, a, pltpu.roll(b, 32, 1)))
            out.append(jnp.where(even, pltpu.roll(a, 96, 1), b))
        return out

    for c in range(2):
        for g in range(2):
            for t in range(4):
                v = regroup([r1[NH * c + 4 * t + i, :, 128 * g:128 * g + 128] for i in range(4)])
                for i in range(4):
                    row = 16 * (8 * c + 4 * g + i)
                    hi, lo = split(v[i])
                    ah[row:row + 16, 128 * t:128 * t + 128] = hi
                    al[row:row + 16, 128 * t:128 * t + 128] = lo
    for n in range(2):
        cols = (hhi[:, 256 * n:256 * n + 256], hlo[:, 256 * n:256 * n + 256])
        o = dot3((ah[...], al[...]), cols)
        fz[:, :, 256 * n:256 * n + 256] = (o * (1.0 / (N * N))).reshape(ZB, 16, 256)

    def down(i, v):
        k = inv_d[base + i]
        v = fz[i] * k + (cpl[base + i] * k) * v
        gd[i] = v
        return v

    def upward(n, v):
        i = ZB - 1 - n
        k = inv_u[base + i]
        return fz[i] * k + (cpl[base + i + 1] * k) * v

    send_a[0] = lax.fori_loop(0, ZB, down, blank, unroll=4)
    send_a[1] = lax.fori_loop(0, ZB, upward, blank, unroll=4)

    def copy2(j, origin):
        to = lax.rem(chip + j, NX_CHIPS)
        return pltpu.make_async_remote_copy(
            src_ref=send_a.at[jnp.where(to > chip, 0, 1)], dst_ref=recv_a.at[origin],
            send_sem=s2.at[j], recv_sem=q2.at[j], device_id=dev(h, 2 * to + core))

    for j in (2, 1, 3):
        copy2(j, chip).start()

    def left2(j, _):
        copy2(j, chip).wait_send()
        return 0

    drains["2"] = lambda: lax.fori_loop(1, NX_CHIPS, left2, 0)
    recv_a[chip] = blank

    def done2(j, _):
        copy2(j, lax.rem(chip + NX_CHIPS - j, NX_CHIPS)).wait_recv()
        return 0

    lax.fori_loop(1, NX_CHIPS, done2, 0)
    from_top, from_bottom = blank, blank
    for j in range(NX_CHIPS - 1):
        from_top = jnp.where(j < chip, recv_a[j] + prod_d[j] * from_top, from_top)
        k = NX_CHIPS - 1 - j
        from_bottom = jnp.where(k > chip, recv_a[k] + prod_u[k] * from_bottom, from_bottom)

    def solved(i, p):
        row = pl.ds(pl.multiple_of(16 * i, 16), 16)
        hi, lo = split(p)
        ah[row, :] = hi
        al[row, :] = lo

    p = (gd[ZB - 1] + pi[ZB - 1] * from_top + r_last * from_bottom) * join
    solved(ZB - 1, p)

    def up(n, p):
        i = ZB - 2 - n
        p = gd[i] + pi[i] * from_top + (cpl[base + i + 1] * inv_d[base + i]) * p
        solved(i, p)
        return p

    lax.fori_loop(0, ZB - 1, up, p)
    for n in range(2):
        cols = (hhi[:, 256 * n:256 * n + 256], hlo[:, 256 * n:256 * n + 256])
        fz[:, :, 256 * n:256 * n + 256] = dot3((ah[...], al[...]), cols).reshape(ZB, 16, 256)
    for c in range(2):
        for g in range(2):
            for t in range(4):
                v = regroup([fz[8 * c + 4 * g + i, :, 128 * t:128 * t + 128] for i in range(4)])
                for i in range(4):
                    w1[NH * c + 4 * t + i, :, 128 * g:128 * g + 128] = v[i]

    def copy4(j, oq):
        pq, fh, fc = fellow(j)
        return pltpu.make_async_remote_copy(
            src_ref=w1.at[slot(pq)], dst_ref=y4.at[oq],
            send_sem=s4.at[j], recv_sem=q4.at[j], device_id=dev(fh, 2 * chip + fc))

    def go4():
        for j in range(NQ - 1):
            copy4(j, q).start()

    go4()

    def left4():
        for j in range(NQ - 1):
            copy4(j, q).wait_send()

    drains["4"] = left4
    y4[q] = w1[slot(q)]

    del drains["c01"], drains["c28"]
    for f, ref in conc:
        for c in halo_copies(f, ref, range(8)):
            c.wait()
        unpack_rows(f, ref)
    for c in vent_copies:
        c.wait()
    ev[XL:XE] = jnp.where(sub8 < 4, vin[1], vin[0])

    for j in range(NQ - 1):
        copy4(j, fellow(j, -1)[0]).wait_recv()

    s = split(y4[...].reshape(N, ZL * XL).T)
    for n in range(2):
        o = dot3(s, (hhi[:, 256 * n:256 * n + 256], hlo[:, 256 * n:256 * n + 256]))
        ep[HALO:HALO + ZL, 0:32, 256 * n:256 * n + 256] = o.reshape(ZL, XL, 256)
    outs = [pltpu.make_async_copy(ep.at[pl.ds(HALO, ZL), pl.ds(0, XL)], out_p, lsem.at[8])]
    outs[0].start()
    drains["out"] = lambda: [c.wait() for c in outs]

    near = halo_copies(0, ep, (8, 9, 2, 3))
    rest = halo_copies(0, ep, (10, 11, 4, 5, 6, 7))
    for c in near[:2]:
        c.start()
    pack_rows(0, ep)
    for c in near[2:] + rest:
        c.start()
    drains["p"] = lambda: [c.wait_send() for c in near + rest]
    drains["pr"] = lambda: [c.wait_recv() for c in rest]
    def cell(i):
        gz = lax.rem(d * ZL + i + (NZ - HALO), NZ)
        kh, cu, cd = khs[gz], cpl[gz], cpl[gz + 1]
        p = ep[i]
        east = -kh * (pltpu.roll(p, XE - 1, 0) - p)
        north = -kh * (pltpu.roll(p, N - 1, 1) - p)
        above = -cu * (p - ep[i - 1])
        below = -cd * (ep[i + 1] - p)
        return east, pltpu.roll(east, 1, 0), north, pltpu.roll(north, 1, 1), above, below

    def speed(*rows):
        def body(i, m):
            e, w, n, s_, a, c = [jnp.abs(v) for v in cell(i)]
            v = e + w + n + s_ + a + c
            for r in rows:
                for k in range(0, N, 128):
                    m = jnp.maximum(m, v[r:r + 8, k:k + 128])
            return m

        return body

    inner = (HALO + 1, HALO + ZL - 1)
    m = lax.fori_loop(*inner, speed(8, 16), jnp.zeros((8, 128), F32))
    for c in near:
        c.wait_recv()
    unpack_rows(0, ep, (2, 3, 4, 5))

    m = lax.fori_loop(*inner, speed(0, 24), m)
    for i in (HALO, HALO + ZL - 1):
        m = speed(0, 8, 16, 24)(i, m)
    mx[0] = m

    def copy_m(j, origin):
        return pltpu.make_async_remote_copy(
            src_ref=mx.at[0], dst_ref=mxh.at[origin], send_sem=ms.at[j], recv_sem=mq.at[j],
            device_id=dev(mate(j), d))

    def copy_n(j, origin):
        return pltpu.make_async_remote_copy(
            src_ref=mx.at[1], dst_ref=mxd.at[origin], send_sem=ns.at[j], recv_sem=nq.at[j],
            device_id=dev(h, lax.rem(d + j, ND)))

    def go_m(j, _):
        copy_m(j, h).start()
        return 0

    lax.fori_loop(1, NH, go_m, 0)
    def left_m(j, _):
        copy_m(j, h).wait_send()
        return 0
    drains["m"] = lambda: lax.fori_loop(1, NH, left_m, 0)
    mxh[h] = mx[0]

    def stencil(get, c_ref, i):
        c = c_ref[i]
        return (get(0) * c
                + get(1) * pltpu.roll(c, XE - 1, 0) + get(2) * pltpu.roll(c, 1, 0)
                + get(3) * pltpu.roll(c, N - 1, 1) + get(4) * pltpu.roll(c, 1, 1)
                + get(5) * c_ref[i + 1] + get(6) * c_ref[i - 1])

    def tendencies(m_ref, s_ref, i):
        get = lambda k: coef[k, i - 1]
        react = REACTION * m_ref[i] * s_ref[i]
        return (stencil(get, m_ref, i) + (react - VENT_INPUT * ev[...]),
                stencil(get, s_ref, i) + react)

    def prepare(i, _):
        e, w, n, s_, a, c = cell(i)
        pos, neg = (lambda v: jnp.maximum(v, 0.0)), (lambda v: jnp.minimum(v, 0.0))
        coef[0, i - 1] = (pos(e) - neg(w)) + (pos(n) - neg(s_)) + (pos(c) - neg(a))
        coef[1, i - 1] = neg(e)
        coef[2, i - 1] = -pos(w)
        coef[3, i - 1] = neg(n)
        coef[4, i - 1] = -pos(s_)
        coef[5, i - 1] = neg(c)
        coef[6, i - 1] = -pos(a)
        t_m, t_s = tendencies(em, es, i)
        tend[0, i - 1] = t_m
        tend[1, i - 1] = t_s
        return 0

    def bend(i, _):
        get = lambda k: coef[k, i - 1]
        curve[0, i - 2] = stencil(get, tend.at[0], i - 1)
        curve[1, i - 2] = stencil(get, tend.at[1], i - 1)
        return 0

    lax.fori_loop(HALO + 1, HALO + ZL - 1, prepare, 0)
    drains.pop("pr")()
    unpack_rows(0, ep, (0, 1, 6, 7))
    lax.fori_loop(1, HALO + 1, prepare, 0)
    lax.fori_loop(HALO + ZL - 1, ZE - 1, prepare, 0)

    def done_m(j, _):
        copy_m(j, lax.rem(h + NH - j, NH)).wait_recv()
        return 0

    lax.fori_loop(1, NH, done_m, 0)
    mx[1] = jnp.max(mxh[...], axis=0)

    def go_n(j, _):
        copy_n(j, d).start()
        return 0

    lax.fori_loop(1, ND, go_n, 0)
    def left_n(j, _):
        copy_n(j, d).wait_send()
        return 0
    drains["n"] = lambda: lax.fori_loop(1, ND, left_n, 0)
    mxd[d] = mx[1]

    lax.fori_loop(2, ZE - 2, bend, 0)

    def done_n(j, _):
        copy_n(j, lax.rem(d + ND - j, ND)).wait_recv()
        return 0

    lax.fori_loop(1, ND, done_n, 0)
    fastest = jnp.max(jnp.max(mxd[...], axis=0), axis=(0, 1), keepdims=True)
    dt = COURANT / (fastest + 1e-6)

    def first(i, _):
        m, s, t_m, t_s = em[i], es[i], tend[0, i - 1], tend[1, i - 1]
        m1, s1 = m - dt * t_m, s - dt * t_s
        more = REACTION * (m1 * s1) - REACTION * (m * s)
        em2[i] = m1 - dt * ((t_m + more) - dt * curve[0, i - 2])
        es2[i] = s1 - dt * ((t_s + more) - dt * curve[1, i - 2])
        return 0

    lax.fori_loop(2, ZE - 2, first, 0)

    def step(a, c, lo):
        def body(i, _):
            t_m, t_s = tendencies(a[0], a[1], i)
            c[0][i] = a[0][i] - dt * t_m
            c[1][i] = a[1][i] - dt * t_s
            return 0

        lax.fori_loop(lo, ZE - lo, body, 0)

    step((em2, es2), (em, es), 3)

    def last(i, _):
        t_m, t_s = tendencies(em, es, i)
        res_m[i - HALO] = (em[i] - dt * t_m)[0:32]
        res_s[i - HALO] = (es[i] - dt * t_s)[0:32]
        return 0

    for part in range(2):
        half = ZL // 2
        lax.fori_loop(HALO + half * part, HALO + half * (part + 1), last, 0)
        at = pl.ds(half * part, half)
        for k, (ref, out) in enumerate(((res_m, out_m), (res_s, out_s))):
            outs.append(pltpu.make_async_copy(ref.at[at], out.at[at], lsem.at[9 + 2 * part + k]))
            outs[-1].start()
    for f in drains.values():
        f()


def deliver(*refs):
    ins, outs, (buf, sem_in, sem_out) = refs[:3], refs[3:6], refs[6:]
    part = ZL // PARTS
    moves = []
    for k in range(3):
        for n in range(PARTS):
            at = pl.ds(n * part, part)
            moves.append((
                pltpu.make_async_copy(ins[k].at[at], buf.at[k, at], sem_in.at[k, n]),
                pltpu.make_async_copy(buf.at[k, at], outs[k].at[at], sem_out.at[k, n])))
    for a, _ in moves:
        a.start()
    for a, b in moves:
        a.wait()
        b.start()
    for _, b in moves:
        b.wait()


def local(source_field, methane, sulfate, layer_of_cell, perm_horizontal, perm_vertical, vent_mask):
    hi, lo, eig_x, eig_y = tables()
    hbm = pl.BlockSpec(memory_space=pl.ANY)
    field = jax.ShapeDtypeStruct((ZL, XL, N), F32)
    dma = pltpu.SemaphoreType.DMA
    ext = pltpu.VMEM((ZE, XE, N), F32)
    scratch = [
        pltpu.VMEM((ZL, XL, N), F32),
        pltpu.VMEM((XL, N), jnp.int32),
        pltpu.VMEM((N, N), BF16),
        pltpu.VMEM((N, N), BF16),
        pltpu.VMEM((16, N), F32),
        pltpu.VMEM((ZL, XL, N), F32),
        pltpu.VMEM((ZL, XL, N), F32),
        pltpu.SMEM((NZ,), jnp.int32),
        pltpu.SMEM((8,), F32),
        pltpu.SMEM((8,), F32),
        pltpu.VMEM((NQ, 16, ZL * XL), F32),
        pltpu.VMEM((NQ, 16, ZL * XL), F32),
        pltpu.VMEM((ZB * 16, N), BF16),
        pltpu.VMEM((ZB * 16, N), BF16),
        pltpu.VMEM((ZB, 16, N), F32),
        pltpu.VMEM((NQ, 16, ZL * XL), F32),
        pltpu.VMEM((NQ, 16, ZL * XL), F32),
        pltpu.VMEM((16, 128), F32),
        pltpu.VMEM((NZ, 16, N), F32),
        pltpu.VMEM((NZ, 16, N), F32),
        pltpu.VMEM((NX_CHIPS, 16, N), F32),
        pltpu.VMEM((NX_CHIPS, 16, N), F32),
        pltpu.VMEM((ZB, 16, N), F32),
        pltpu.VMEM((ZB, 16, N), F32),
        pltpu.VMEM((2, 16, N), F32),
        pltpu.VMEM((NX_CHIPS, 16, N), F32),
        ext, ext, ext, ext, ext,
        pltpu.VMEM((XE, N), F32),
        pltpu.VMEM((2, 8, N), F32),
        pltpu.VMEM((3, 2, ZL // 2, 8, N), F32),
        pltpu.VMEM((3, 2, ZE // 2, 8, N), F32),
        pltpu.VMEM((7, ZE - 2, XE, N), F32),
        pltpu.VMEM((2, ZE - 2, XE, N), F32),
        pltpu.VMEM((2, ZE - 4, XE, N), F32),
        pltpu.VMEM((2, 8, 128), F32),
        pltpu.VMEM((NH, 8, 128), F32),
        pltpu.VMEM((ND, 8, 128), F32),
        pltpu.SMEM((NZ + 1,), F32),
        pltpu.SMEM((NZ,), F32),
        dma((NQ,)), dma((NQ,)), dma((NX_CHIPS,)), dma((NX_CHIPS,)), dma((NQ,)), dma((NQ,)),
        dma((3, 12)), dma((3, 12)), dma((2,)), dma((2,)),
        dma((NH,)), dma((NH,)), dma((ND,)), dma((ND,)), dma((16,)),
    ]
    results = pl.pallas_call(
        kernel,
        out_shape=(field, field, field),
        in_specs=[hbm] * 11,
        out_specs=(hbm, hbm, hbm),
        scratch_shapes=scratch,
        compiler_params=pltpu.CompilerParams(
            collective_id=0, has_side_effects=True, vmem_limit_bytes=60 * 1024 * 1024),
    )(source_field, methane, sulfate, layer_of_cell, perm_horizontal, perm_vertical, vent_mask,
      jnp.asarray(hi), jnp.asarray(lo), jnp.asarray(eig_x), jnp.asarray(eig_y))
    return pl.pallas_call(
        deliver,
        out_shape=(field, field, field),
        in_specs=[hbm] * 3,
        out_specs=(hbm,) * 3,
        scratch_shapes=[pltpu.VMEM((3, ZL, XL, N), F32), dma((3, PARTS)), dma((3, PARTS))],
    )(*results)


def solution(mesh):
    field = P("depth", "horiz", None)
    return jax.shard_map(
        local,
        mesh=mesh,
        in_specs=(field, field, field, P(), P(), P(), P("horiz", None)),
        out_specs=(field, field, field),
        check_vma=False,
    )
```

```python
import jax
import jax.numpy as jnp
import ml_dtypes
import numpy as np
from jax import lax
from jax.experimental import pallas as pl
from jax.experimental.pallas import tpu as pltpu
from jax.sharding import PartitionSpec as P

STEPS = 4
STORAGE = 0.004
COURANT = 0.5
REACTION = 4.0
VENT_INPUT = 4.0

NZ = 64
N = 512
NH = 16
ND = 8
ZL = 8
XL = 32
HALO = 4
ZE = ZL + 2 * HALO
XE = XL + 2 * HALO
NX_CHIPS = 4
ZB = NZ // NX_CHIPS
NQ = 2 * NH

PLANE = sorted(
    [(z, y, c) for z in range(4) for y in range(4) for c in range(2)][1:],
    key=lambda o: -(min(o[0], 4 - o[0]) + min(o[1], 4 - o[1])))

PARTS = 2

F32 = jnp.float32
BF16 = jnp.bfloat16


def tables():
    k = np.arange(N)
    angle = (k[:, None] * k[None, :] % N) * (2.0 * np.pi / N)
    cas = np.cos(angle) + np.sin(angle)
    hi = cas.astype(np.float32).astype(ml_dtypes.bfloat16)
    lo = (cas - hi.astype(np.float64)).astype(np.float32).astype(ml_dtypes.bfloat16)
    eig = (4.0 * np.sin(np.pi * k / N) ** 2).astype(np.float32)
    eig_x = np.broadcast_to(eig.reshape(1, N), (16, N)).copy()
    eig_y = np.broadcast_to(eig.reshape(NQ, 16, 1), (NQ, 16, 128)).copy()
    return hi, lo, eig_x, eig_y


def split(v):
    hi = v.astype(BF16)
    return hi, (v - hi.astype(F32)).astype(BF16)


def dot3(a, b, dims=((1,), (0,))):
    (ah, al), (bh, bl) = a, b
    d = lambda x, y: lax.dot_general(x, y, (dims, ((), ())), preferred_element_type=F32)
    return d(ah, bh) + (d(al, bh) + d(ah, bl))


def kernel(
    src_in, met, sul, layer_in, ph_in, pv_in, vent_in, hhi_in, hlo_in, eig_x_in, eig_y,
    out_p, out_m, out_s,
    src, vent, hhi, hlo, eig_x, res_m, res_s, layer, ph, pv,
    y1, r1, ah, al, fz, w1, y4, ey,
    inv_d, inv_u, prod_d, prod_u, gd, pi, send_a, recv_a,
    ep, em, es, em2, es2, ev, vin, pack, xin, coef, tend, curve,
    mx, mxh, mxd, cpl, khs,
    s1, q1, s2, q2, s4, q4, hs, hq, vs, vq, ms, mq, ns, nq, lsem,
):
    h = lax.axis_index("horiz")
    d = lax.axis_index("depth")
    chip = lax.div(d, 2)
    core = lax.rem(d, 2)
    q = h * 2 + core

    drains = {}

    def dev(hh, dd):
        return {"horiz": hh, "depth": dd}

    def mate(j):
        return lax.rem(h + j, NH)

    hz, hy = lax.div(h, 4), lax.rem(h, 4)

    def fellow(j, sign=1):
        dz, dy, dc = PLANE[j]
        fh = lax.rem(hz + sign * dz + 4, 4) * 4 + lax.rem(hy + sign * dy + 4, 4)
        fc = lax.rem(core + dc, 2)
        return 2 * fh + fc, fh, fc

    def slot(oq):
        return lax.rem(oq, 2) * NH + lax.div(oq, 2)

    h_up, h_dn = lax.rem(h + 1, NH), lax.rem(h + NH - 1, NH)
    d_up, d_dn = lax.rem(d + 1, ND), lax.rem(d + ND - 1, ND)

    first_loads = [
        pltpu.make_async_copy(src_in, src, lsem.at[3]),
        pltpu.make_async_copy(hhi_in, hhi, lsem.at[4]),
        pltpu.make_async_copy(hlo_in, hlo, lsem.at[5]),
    ]
    for c in first_loads:
        c.start()

    barrier = pltpu.get_barrier_semaphore()

    for j in range(NQ - 1):
        _, fh, fc = fellow(j)
        pl.semaphore_signal(barrier, inc=1, device_id=dev(fh, 2 * chip + fc))

    def greet_d(j, _):
        pl.semaphore_signal(barrier, inc=1, device_id=dev(h, lax.rem(d + j, ND)))
        return 0

    lax.fori_loop(1, ND, greet_d, 0)
    for hh in (h_up, h_dn):
        for dd in (d_up, d_dn):
            pl.semaphore_signal(barrier, inc=1, device_id=dev(hh, dd))

    own_copies = [
        pltpu.make_async_copy(met, em.at[pl.ds(HALO, ZL), pl.ds(0, XL)], lsem.at[0]),
        pltpu.make_async_copy(sul, es.at[pl.ds(HALO, ZL), pl.ds(0, XL)], lsem.at[1]),
        pltpu.make_async_copy(eig_y.at[q], ey, lsem.at[2]),
        pltpu.make_async_copy(vent_in, vent, lsem.at[6]),
        pltpu.make_async_copy(eig_x_in, eig_x, lsem.at[7]),
        pltpu.make_async_copy(layer_in, layer, lsem.at[13]),
        pltpu.make_async_copy(ph_in, ph, lsem.at[14]),
        pltpu.make_async_copy(pv_in, pv, lsem.at[15]),
    ]
    for c in own_copies:
        c.start()
    drains["own"] = lambda: [c.wait() for c in own_copies]

    for c in first_loads:
        c.wait()
    s = split(src[...].reshape(ZL * XL, N))
    for n in range(2):
        rows = (hhi[256 * n:256 * n + 256], hlo[256 * n:256 * n + 256])
        y1[16 * n:16 * n + 16] = dot3(rows, s, ((1,), (1,))).reshape(16, 16, ZL * XL)

    pl.semaphore_wait(barrier, (NQ - 1) + (ND - 1) + 4)

    def copy1(j, oq):
        pq, fh, fc = fellow(j)
        return pltpu.make_async_remote_copy(
            src_ref=y1.at[pq], dst_ref=r1.at[slot(oq)],
            send_sem=s1.at[j], recv_sem=q1.at[j], device_id=dev(fh, 2 * chip + fc))

    def go1():
        for j in range(NQ - 1):
            copy1(j, q).start()

    go1()
    def left1():
        for j in range(NQ - 1):
            copy1(j, q).wait_send()
    drains["1"] = left1

    def halo_copies(f, ref, dirs):
        own = pl.ds(0, XL)
        lo_p, hi_p = pack.at[f, 0], pack.at[f, 1]
        plan = (
            (ref.at[pl.ds(8, 4), own], ref.at[pl.ds(0, 4), own], h, d_up),
            (ref.at[pl.ds(4, 4), own], ref.at[pl.ds(12, 4), own], h, d_dn),
            (hi_p, xin.at[f, 0, pl.ds(2, 4)], h_up, d),
            (lo_p, xin.at[f, 1, pl.ds(2, 4)], h_dn, d),
            (hi_p.at[pl.ds(2, 2)], xin.at[f, 0, pl.ds(0, 2)], h_up, d_up),
            (hi_p.at[pl.ds(0, 2)], xin.at[f, 0, pl.ds(6, 2)], h_up, d_dn),
            (lo_p.at[pl.ds(2, 2)], xin.at[f, 1, pl.ds(0, 2)], h_dn, d_up),
            (lo_p.at[pl.ds(0, 2)], xin.at[f, 1, pl.ds(6, 2)], h_dn, d_dn),
            (ref.at[pl.ds(11, 1), own], ref.at[pl.ds(3, 1), own], h, d_up),
            (ref.at[pl.ds(4, 1), own], ref.at[pl.ds(12, 1), own], h, d_dn),
            (ref.at[pl.ds(8, 3), own], ref.at[pl.ds(0, 3), own], h, d_up),
            (ref.at[pl.ds(5, 3), own], ref.at[pl.ds(13, 3), own], h, d_dn),
        )
        return [
            pltpu.make_async_remote_copy(
                src_ref=plan[i][0], dst_ref=plan[i][1], send_sem=hs.at[f, i], recv_sem=hq.at[f, i],
                device_id=dev(plan[i][2], plan[i][3]))
            for i in dirs
        ]

    sub8 = lax.broadcasted_iota(jnp.int32, (8, N), 0)

    def pack_rows(f, ref):
        for zz in range(ZL // 2):
            even, odd = ref[HALO + 2 * zz], ref[HALO + 2 * zz + 1]
            pack[f, 0, zz] = jnp.where(sub8 < 4, even[0:8], pltpu.roll(odd[0:8], 4, 0))
            pack[f, 1, zz] = jnp.where(sub8 >= 4, even[24:32], pltpu.roll(odd[24:32], 4, 0))

    def unpack_rows(f, ref, pairs=range(ZE // 2)):
        for zz in pairs:
            lower, upper = xin[f, 0, zz], xin[f, 1, zz]
            ref[2 * zz, XL:XE] = jnp.where(sub8 < 4, upper, lower)
            ref[2 * zz + 1, XL:XE] = pltpu.roll(jnp.where(sub8 < 4, lower, upper), 4, 0)

    drains.pop("own")()
    conc = ((1, em), (2, es))
    for f, ref in conc:
        for c in halo_copies(f, ref, (0, 1)):
            c.start()
    drains["c01"] = lambda: [c.wait() for f, ref in conc for c in halo_copies(f, ref, (0, 1))]
    for f, ref in conc:
        pack_rows(f, ref)
    ev[0:32] = vent[...].astype(F32)
    vent_copies = [
        pltpu.make_async_remote_copy(
            src_ref=ev.at[pl.ds(24, 8)], dst_ref=vin.at[0],
            send_sem=vs.at[0], recv_sem=vq.at[0], device_id=dev(h_up, d)),
        pltpu.make_async_remote_copy(
            src_ref=ev.at[pl.ds(0, 8)], dst_ref=vin.at[1],
            send_sem=vs.at[1], recv_sem=vq.at[1], device_id=dev(h_dn, d)),
    ]

    def table(z, _):
        khs[z] = ph[layer[z]]
        return 0

    lax.fori_loop(0, NZ, table, 0)
    cpl[0] = 0.0
    cpl[NZ] = 0.0

    def face(i, _):
        a, c = pv[layer[i - 1]], pv[layer[i]]
        cpl[i] = 2.0 * a * c / (a + c)
        return 0

    lax.fori_loop(1, NZ, face, 0)

    lam = eig_x[...] + jnp.concatenate([ey[...]] * 4, axis=1)
    blank = jnp.zeros((16, N), F32)
    state = (blank, blank)
    for j in range(NX_CHIPS):
        def factor(i, carry, j=j):
            rd, ru, bd, bu = carry
            z, y = ZB * j + i, NZ - 1 - ZB * j - i
            cu, cd = cpl[z], cpl[z + 1]
            v = 1.0 / ((cu + cd + khs[z] * lam + STORAGE) - cu * rd)
            inv_d[z] = v
            rd, bd = cd * v, bd * (cu * v)
            cu, cd = cpl[y], cpl[y + 1]
            v = 1.0 / ((cu + cd + khs[y] * lam + STORAGE) - cd * ru)
            inv_u[y] = v
            ru, bu = cu * v, bu * (cd * v)
            return rd, ru, bd, bu

        rd, ru, bd, bu = lax.fori_loop(0, ZB, factor, state + (blank + 1.0, blank + 1.0))
        state = (rd, ru)
        prod_d[j] = bd
        prod_u[NX_CHIPS - 1 - j] = bu
    base = ZB * chip

    def product(i, v):
        v = v * (cpl[base + i] * inv_d[base + i])
        pi[i] = v
        return v

    lax.fori_loop(0, ZB, product, blank + 1.0)
    r_last = cpl[base + ZB] * inv_d[base + ZB - 1]
    r_next = cpl[base + ZB] * inv_u[jnp.minimum(base + ZB, NZ - 1)]
    join = 1.0 / (1.0 - r_last * r_next)

    r1[slot(q)] = y1[q]

    for j in range(8):
        copy1(j, fellow(j, -1)[0]).wait_recv()
    for f, ref in conc:
        for c in halo_copies(f, ref, range(2, 8)):
            c.start()
    for c in vent_copies:
        c.start()
    drains["c28"] = lambda: [c.wait() for c in vent_copies + [c for f, ref in conc for c in halo_copies(f, ref, range(2, 8))]]

    for j in range(8, NQ - 1):
        copy1(j, fellow(j, -1)[0]).wait_recv()
    group = lax.broadcasted_iota(jnp.int32, (16, 128), 1) // 32

    def regroup(v):
        lower, even = group < 2, lax.rem(group, 2) == 0
        p = [jnp.where(lower, v[i], pltpu.roll(v[i + 2], 64, 1)) for i in range(2)]
        r = [jnp.where(lower, pltpu.roll(v[i], 64, 1), v[i + 2]) for i in range(2)]
        out = []
        for a, b in (p, r):
            out.append(jnp.where(even, a, pltpu.roll(b, 32, 1)))
            out.append(jnp.where(even, pltpu.roll(a, 96, 1), b))
        return out

    for c in range(2):
        for g in range(2):
            for t in range(4):
                v = regroup([r1[NH * c + 4 * t + i, :, 128 * g:128 * g + 128] for i in range(4)])
                for i in range(4):
                    row = 16 * (8 * c + 4 * g + i)
                    hi, lo = split(v[i])
                    ah[row:row + 16, 128 * t:128 * t + 128] = hi
                    al[row:row + 16, 128 * t:128 * t + 128] = lo
    for n in range(2):
        cols = (hhi[:, 256 * n:256 * n + 256], hlo[:, 256 * n:256 * n + 256])
        o = dot3((ah[...], al[...]), cols)
        fz[:, :, 256 * n:256 * n + 256] = (o * (1.0 / (N * N))).reshape(ZB, 16, 256)

    def down(i, v):
        k = inv_d[base + i]
        v = fz[i] * k + (cpl[base + i] * k) * v
        gd[i] = v
        return v

    def upward(n, v):
        i = ZB - 1 - n
        k = inv_u[base + i]
        return fz[i] * k + (cpl[base + i + 1] * k) * v

    send_a[0] = lax.fori_loop(0, ZB, down, blank, unroll=4)
    send_a[1] = lax.fori_loop(0, ZB, upward, blank, unroll=4)

    def copy2(j, origin):
        to = lax.rem(chip + j, NX_CHIPS)
        return pltpu.make_async_remote_copy(
            src_ref=send_a.at[jnp.where(to > chip, 0, 1)], dst_ref=recv_a.at[origin],
            send_sem=s2.at[j], recv_sem=q2.at[j], device_id=dev(h, 2 * to + core))

    for j in (2, 1, 3):
        copy2(j, chip).start()

    def left2(j, _):
        copy2(j, chip).wait_send()
        return 0

    drains["2"] = lambda: lax.fori_loop(1, NX_CHIPS, left2, 0)
    recv_a[chip] = blank

    def done2(j, _):
        copy2(j, lax.rem(chip + NX_CHIPS - j, NX_CHIPS)).wait_recv()
        return 0

    lax.fori_loop(1, NX_CHIPS, done2, 0)
    from_top, from_bottom = blank, blank
    for j in range(NX_CHIPS - 1):
        from_top = jnp.where(j < chip, recv_a[j] + prod_d[j] * from_top, from_top)
        k = NX_CHIPS - 1 - j
        from_bottom = jnp.where(k > chip, recv_a[k] + prod_u[k] * from_bottom, from_bottom)

    def solved(i, p):
        row = pl.ds(pl.multiple_of(16 * i, 16), 16)
        hi, lo = split(p)
        ah[row, :] = hi
        al[row, :] = lo

    p = (gd[ZB - 1] + pi[ZB - 1] * from_top + r_last * from_bottom) * join
    solved(ZB - 1, p)

    def up(n, p):
        i = ZB - 2 - n
        p = gd[i] + pi[i] * from_top + (cpl[base + i + 1] * inv_d[base + i]) * p
        solved(i, p)
        return p

    lax.fori_loop(0, ZB - 1, up, p)
    for n in range(2):
        cols = (hhi[:, 256 * n:256 * n + 256], hlo[:, 256 * n:256 * n + 256])
        fz[:, :, 256 * n:256 * n + 256] = dot3((ah[...], al[...]), cols).reshape(ZB, 16, 256)
    for c in range(2):
        for g in range(2):
            for t in range(4):
                v = regroup([fz[8 * c + 4 * g + i, :, 128 * t:128 * t + 128] for i in range(4)])
                for i in range(4):
                    w1[NH * c + 4 * t + i, :, 128 * g:128 * g + 128] = v[i]

    def copy4(j, oq):
        pq, fh, fc = fellow(j)
        return pltpu.make_async_remote_copy(
            src_ref=w1.at[slot(pq)], dst_ref=y4.at[oq],
            send_sem=s4.at[j], recv_sem=q4.at[j], device_id=dev(fh, 2 * chip + fc))

    def go4():
        for j in range(NQ - 1):
            copy4(j, q).start()

    go4()

    def left4():
        for j in range(NQ - 1):
            copy4(j, q).wait_send()

    drains["4"] = left4
    y4[q] = w1[slot(q)]

    del drains["c01"], drains["c28"]
    for f, ref in conc:
        for c in halo_copies(f, ref, range(8)):
            c.wait()
        unpack_rows(f, ref)
    for c in vent_copies:
        c.wait()
    ev[XL:XE] = jnp.where(sub8 < 4, vin[1], vin[0])

    for j in range(NQ - 1):
        copy4(j, fellow(j, -1)[0]).wait_recv()

    s = split(y4[...].reshape(N, ZL * XL).T)
    for n in range(2):
        o = dot3(s, (hhi[:, 256 * n:256 * n + 256], hlo[:, 256 * n:256 * n + 256]))
        ep[HALO:HALO + ZL, 0:32, 256 * n:256 * n + 256] = o.reshape(ZL, XL, 256)
    outs = [pltpu.make_async_copy(ep.at[pl.ds(HALO, ZL), pl.ds(0, XL)], out_p, lsem.at[8])]
    outs[0].start()
    drains["out"] = lambda: [c.wait() for c in outs]

    near = halo_copies(0, ep, (8, 9, 2, 3))
    rest = halo_copies(0, ep, (10, 11, 4, 5, 6, 7))
    for c in near[:2]:
        c.start()
    pack_rows(0, ep)
    for c in near[2:] + rest:
        c.start()
    drains["p"] = lambda: [c.wait_send() for c in near + rest]
    drains["pr"] = lambda: [c.wait_recv() for c in rest]
    def cell(i):
        gz = lax.rem(d * ZL + i + (NZ - HALO), NZ)
        kh, cu, cd = khs[gz], cpl[gz], cpl[gz + 1]
        p = ep[i]
        east = -kh * (pltpu.roll(p, XE - 1, 0) - p)
        north = -kh * (pltpu.roll(p, N - 1, 1) - p)
        above = -cu * (p - ep[i - 1])
        below = -cd * (ep[i + 1] - p)
        return east, pltpu.roll(east, 1, 0), north, pltpu.roll(north, 1, 1), above, below

    def speed(*rows):
        def body(i, m):
            e, w, n, s_, a, c = [jnp.abs(v) for v in cell(i)]
            v = e + w + n + s_ + a + c
            for r in rows:
                for k in range(0, N, 128):
                    m = jnp.maximum(m, v[r:r + 8, k:k + 128])
            return m

        return body

    inner = (HALO + 1, HALO + ZL - 1)
    m = lax.fori_loop(*inner, speed(8, 16), jnp.zeros((8, 128), F32))
    for c in near:
        c.wait_recv()
    unpack_rows(0, ep, (2, 3, 4, 5))

    m = lax.fori_loop(*inner, speed(0, 24), m)
    for i in (HALO, HALO + ZL - 1):
        m = speed(0, 8, 16, 24)(i, m)
    mx[0] = m

    def copy_m(j, origin):
        return pltpu.make_async_remote_copy(
            src_ref=mx.at[0], dst_ref=mxh.at[origin], send_sem=ms.at[j], recv_sem=mq.at[j],
            device_id=dev(mate(j), d))

    def copy_n(j, origin):
        return pltpu.make_async_remote_copy(
            src_ref=mx.at[1], dst_ref=mxd.at[origin], send_sem=ns.at[j], recv_sem=nq.at[j],
            device_id=dev(h, lax.rem(d + j, ND)))

    def go_m(j, _):
        copy_m(j, h).start()
        return 0

    lax.fori_loop(1, NH, go_m, 0)
    def left_m(j, _):
        copy_m(j, h).wait_send()
        return 0
    drains["m"] = lambda: lax.fori_loop(1, NH, left_m, 0)
    mxh[h] = mx[0]

    def stencil(get, c_ref, i):
        c = c_ref[i]
        return (get(0) * c
                + get(1) * pltpu.roll(c, XE - 1, 0) + get(2) * pltpu.roll(c, 1, 0)
                + get(3) * pltpu.roll(c, N - 1, 1) + get(4) * pltpu.roll(c, 1, 1)
                + get(5) * c_ref[i + 1] + get(6) * c_ref[i - 1])

    def tendencies(m_ref, s_ref, i):
        get = lambda k: coef[k, i - 1]
        react = REACTION * m_ref[i] * s_ref[i]
        return (stencil(get, m_ref, i) + (react - VENT_INPUT * ev[...]),
                stencil(get, s_ref, i) + react)

    def prepare(i, _):
        e, w, n, s_, a, c = cell(i)
        pos, neg = (lambda v: jnp.maximum(v, 0.0)), (lambda v: jnp.minimum(v, 0.0))
        coef[0, i - 1] = (pos(e) - neg(w)) + (pos(n) - neg(s_)) + (pos(c) - neg(a))
        coef[1, i - 1] = neg(e)
        coef[2, i - 1] = -pos(w)
        coef[3, i - 1] = neg(n)
        coef[4, i - 1] = -pos(s_)
        coef[5, i - 1] = neg(c)
        coef[6, i - 1] = -pos(a)
        t_m, t_s = tendencies(em, es, i)
        tend[0, i - 1] = t_m
        tend[1, i - 1] = t_s
        return 0

    def bend(i, _):
        get = lambda k: coef[k, i - 1]
        curve[0, i - 2] = stencil(get, tend.at[0], i - 1)
        curve[1, i - 2] = stencil(get, tend.at[1], i - 1)
        return 0

    lax.fori_loop(HALO + 1, HALO + ZL - 1, prepare, 0)
    drains.pop("pr")()
    unpack_rows(0, ep, (0, 1, 6, 7))
    lax.fori_loop(1, HALO + 1, prepare, 0)
    lax.fori_loop(HALO + ZL - 1, ZE - 1, prepare, 0)

    def done_m(j, _):
        copy_m(j, lax.rem(h + NH - j, NH)).wait_recv()
        return 0

    lax.fori_loop(1, NH, done_m, 0)
    mx[1] = jnp.max(mxh[...], axis=0)

    def go_n(j, _):
        copy_n(j, d).start()
        return 0

    lax.fori_loop(1, ND, go_n, 0)
    def left_n(j, _):
        copy_n(j, d).wait_send()
        return 0
    drains["n"] = lambda: lax.fori_loop(1, ND, left_n, 0)
    mxd[d] = mx[1]

    lax.fori_loop(2, ZE - 2, bend, 0)

    for key in ("1", "2", "4", "p", "m"):
        drains.pop(key)()

    def done_n(j, _):
        copy_n(j, lax.rem(d + ND - j, ND)).wait_recv()
        return 0

    lax.fori_loop(1, ND, done_n, 0)
    fastest = jnp.max(jnp.max(mxd[...], axis=0), axis=(0, 1), keepdims=True)
    dt = COURANT / (fastest + 1e-6)

    def first(i, _):
        m, s, t_m, t_s = em[i], es[i], tend[0, i - 1], tend[1, i - 1]
        m1, s1 = m - dt * t_m, s - dt * t_s
        more = REACTION * (m1 * s1) - REACTION * (m * s)
        em2[i] = m1 - dt * ((t_m + more) - dt * curve[0, i - 2])
        es2[i] = s1 - dt * ((t_s + more) - dt * curve[1, i - 2])
        return 0

    lax.fori_loop(2, ZE - 2, first, 0)

    def step(a, c, lo):
        def body(i, _):
            t_m, t_s = tendencies(a[0], a[1], i)
            c[0][i] = a[0][i] - dt * t_m
            c[1][i] = a[1][i] - dt * t_s
            return 0

        lax.fori_loop(lo, ZE - lo, body, 0)

    step((em2, es2), (em, es), 3)

    def last(i, _):
        t_m, t_s = tendencies(em, es, i)
        res_m[i - HALO] = (em[i] - dt * t_m)[0:32]
        res_s[i - HALO] = (es[i] - dt * t_s)[0:32]
        return 0

    for part in range(2):
        half = ZL // 2
        lax.fori_loop(HALO + half * part, HALO + half * (part + 1), last, 0)
        at = pl.ds(half * part, half)
        for k, (ref, out) in enumerate(((res_m, out_m), (res_s, out_s))):
            outs.append(pltpu.make_async_copy(ref.at[at], out.at[at], lsem.at[9 + 2 * part + k]))
            outs[-1].start()
    for f in drains.values():
        f()


def deliver(*refs):
    ins, outs, (buf, sem_in, sem_out) = refs[:3], refs[3:6], refs[6:]
    part = ZL // PARTS
    moves = []
    for k in range(3):
        for n in range(PARTS):
            at = pl.ds(n * part, part)
            moves.append((
                pltpu.make_async_copy(ins[k].at[at], buf.at[k, at], sem_in.at[k, n]),
                pltpu.make_async_copy(buf.at[k, at], outs[k].at[at], sem_out.at[k, n])))
    for a, _ in moves:
        a.start()
    for a, b in moves:
        a.wait()
        b.start()
    for _, b in moves:
        b.wait()


def local(source_field, methane, sulfate, layer_of_cell, perm_horizontal, perm_vertical, vent_mask):
    hi, lo, eig_x, eig_y = tables()
    hbm = pl.BlockSpec(memory_space=pl.ANY)
    field = jax.ShapeDtypeStruct((ZL, XL, N), F32)
    dma = pltpu.SemaphoreType.DMA
    ext = pltpu.VMEM((ZE, XE, N), F32)
    scratch = [
        pltpu.VMEM((ZL, XL, N), F32),
        pltpu.VMEM((XL, N), jnp.int32),
        pltpu.VMEM((N, N), BF16),
        pltpu.VMEM((N, N), BF16),
        pltpu.VMEM((16, N), F32),
        pltpu.VMEM((ZL, XL, N), F32),
        pltpu.VMEM((ZL, XL, N), F32),
        pltpu.SMEM((NZ,), jnp.int32),
        pltpu.SMEM((8,), F32),
        pltpu.SMEM((8,), F32),
        pltpu.VMEM((NQ, 16, ZL * XL), F32),
        pltpu.VMEM((NQ, 16, ZL * XL), F32),
        pltpu.VMEM((ZB * 16, N), BF16),
        pltpu.VMEM((ZB * 16, N), BF16),
        pltpu.VMEM((ZB, 16, N), F32),
        pltpu.VMEM((NQ, 16, ZL * XL), F32),
        pltpu.VMEM((NQ, 16, ZL * XL), F32),
        pltpu.VMEM((16, 128), F32),
        pltpu.VMEM((NZ, 16, N), F32),
        pltpu.VMEM((NZ, 16, N), F32),
        pltpu.VMEM((NX_CHIPS, 16, N), F32),
        pltpu.VMEM((NX_CHIPS, 16, N), F32),
        pltpu.VMEM((ZB, 16, N), F32),
        pltpu.VMEM((ZB, 16, N), F32),
        pltpu.VMEM((2, 16, N), F32),
        pltpu.VMEM((NX_CHIPS, 16, N), F32),
        ext, ext, ext, ext, ext,
        pltpu.VMEM((XE, N), F32),
        pltpu.VMEM((2, 8, N), F32),
        pltpu.VMEM((3, 2, ZL // 2, 8, N), F32),
        pltpu.VMEM((3, 2, ZE // 2, 8, N), F32),
        pltpu.VMEM((7, ZE - 2, XE, N), F32),
        pltpu.VMEM((2, ZE - 2, XE, N), F32),
        pltpu.VMEM((2, ZE - 4, XE, N), F32),
        pltpu.VMEM((2, 8, 128), F32),
        pltpu.VMEM((NH, 8, 128), F32),
        pltpu.VMEM((ND, 8, 128), F32),
        pltpu.SMEM((NZ + 1,), F32),
        pltpu.SMEM((NZ,), F32),
        dma((NQ,)), dma((NQ,)), dma((NX_CHIPS,)), dma((NX_CHIPS,)), dma((NQ,)), dma((NQ,)),
        dma((3, 12)), dma((3, 12)), dma((2,)), dma((2,)),
        dma((NH,)), dma((NH,)), dma((ND,)), dma((ND,)), dma((16,)),
    ]
    results = pl.pallas_call(
        kernel,
        out_shape=(field, field, field),
        in_specs=[hbm] * 11,
        out_specs=(hbm, hbm, hbm),
        scratch_shapes=scratch,
        compiler_params=pltpu.CompilerParams(
            collective_id=0, has_side_effects=True, vmem_limit_bytes=60 * 1024 * 1024),
    )(source_field, methane, sulfate, layer_of_cell, perm_horizontal, perm_vertical, vent_mask,
      jnp.asarray(hi), jnp.asarray(lo), jnp.asarray(eig_x), jnp.asarray(eig_y))
    return pl.pallas_call(
        deliver,
        out_shape=(field, field, field),
        in_specs=[hbm] * 3,
        out_specs=(hbm,) * 3,
        scratch_shapes=[pltpu.VMEM((3, ZL, XL, N), F32), dma((3, PARTS)), dma((3, PARTS))],
    )(*results)


def solution(mesh):
    field = P("depth", "horiz", None)
    return jax.shard_map(
        local,
        mesh=mesh,
        in_specs=(field, field, field, P(), P(), P(), P("horiz", None)),
        out_specs=(field, field, field),
        check_vma=False,
    )
```
